32 devices in a mesh: fsdp: 8 (over z, y), dp: 4 (over x, core).
Axes of the slice: x: 2, y: 2, z: 4, core: 2. Of those that a mesh axis runs over, the one named last changes fastest.
Arguments:
- patch_acts: bfloat16 [4096, 12288], P(('fsdp', 'dp')), may hold values from -6 to 6
- patch_slot: int32 [4096], P(('fsdp', 'dp')), may hold values from 0 to 256, as said below
- out_grads: bfloat16 [2048, 3072], P(('fsdp', 'dp')), may hold values from -6 to 6
- latent_weight: bfloat16 [12288, 3072], P('dp', 'fsdp'), may hold values from -0.0546875 to 0.0546875
- step_size: bfloat16 [1, 3072], P(None, 'fsdp')
Outputs:
- grad_acts: bfloat16 [4096, 12288], P(('fsdp', 'dp'))
- grad_weight: float32 [12288, 3072], P('dp', 'fsdp')
- grad_step: float32 [1, 3072], P(None, 'fsdp')
The draws below stay inside these ranges and needn't reach their ends.
Inputs may be any that keep to these rules, and one draw needn't show every extreme that they name: `patch_slot`: within each fsdp index, the used patch rows of every image owner come first in its 128 slots and carry a packed row below 256, the others carry 256; each packed row of the fsdp index receives exactly one patch row; in every fsdp index some image owner has all 128 slots used.
All inputs are finite; a program needn't handle non-finite values.
Results may differ from the reference program's by a relative error of at most 0.0049.
Values may be sent and summed in bfloat16 or wider, within the bound.
A program may use at most 128 MiB of HBM per device.

```python
import jax
import jax.numpy as jnp

D_W = 3072
FF_W = 12288
PATCH_CAP = 128
ROWS = 256
ALL_PATCH = 4096
ALL_ROWS = 2048
N_FSDP = 8
N_DP = 4


def draw_step_size(key, part):
    base_step = FF_W ** (-0.5)
    spread = jax.random.uniform(key, (1, D_W), jnp.float32)
    return (base_step * jnp.exp(jnp.log(0.25) + spread * jnp.log(10.0))).astype(jnp.bfloat16)


def draw_patch_slot(key, part):
    half_cap = PATCH_CAP // 2
    group_rows = half_cap * N_DP

    def one_group(group_key):
        first_key, second_key, third_key = jax.random.split(group_key, 3)
        order = jax.random.permutation(first_key, N_DP).astype(jnp.int32)
        extra = jax.random.randint(second_key, (N_DP // 2,), 0, half_cap + 1).astype(jnp.int32)
        extra = extra.at[0].set(half_cap)
        shifted = jnp.zeros((N_DP,), jnp.int32).at[order[0::2]].set(extra).at[order[1::2]].set(-extra)
        counts = half_cap + shifted
        positions = jnp.arange(PATCH_CAP, dtype=jnp.int32)
        valid = (positions[None, :] < counts[:, None]).astype(jnp.int32).reshape(-1)
        ranking = jnp.cumsum(valid) - 1
        shuffled = jax.random.permutation(third_key, group_rows).astype(jnp.int32)
        chosen = shuffled[jnp.clip(ranking, 0, group_rows - 1)]
        return jnp.where(valid == 1, chosen, group_rows).astype(jnp.int32)
    group_keys = jax.random.split(key, N_FSDP)
    return jax.vmap(one_group)(group_keys).reshape(-1).astype(jnp.int32)


def levels(key, shape, shards, low, largest):
    def one(dim, blocks):
        heights = jax.random.uniform(jax.random.fold_in(jax.random.fold_in(key, 6), dim), (blocks,), jnp.float32, low / len(shards), largest / len(shards))
        return jnp.repeat(jnp.exp(heights), shape[dim] // blocks).reshape((-1,) + (1,) * (len(shape) - dim - 1))

    factor_of = one(*shards[0])
    for cut in shards[1:]:
        factor_of = factor_of * one(*cut)
    return factor_of


def scatter_about(stream_key, dims, scale, limit, cuts=(), held_as=jnp.bfloat16):
    array = scale * jax.random.normal(stream_key, dims, jnp.float32)
    if cuts:
        array = array * levels(stream_key, dims, cuts, -0.22, 0.18)
    return jnp.clip(array, -limit, limit).astype(held_as)


def setup_inputs(seed: int = 0) -> dict:
    key_of = jax.random.split(jax.random.key(seed), 6)
    return {
        "patch_acts": scatter_about(key_of[0], (ALL_PATCH, FF_W), 1.0, 6.0, ((0, 32),)),
        "patch_slot": draw_patch_slot(jax.random.fold_in(key_of[5], 71), 0),
        "out_grads": scatter_about(key_of[2], (ALL_ROWS, D_W), 1.0, 6.0, ((0, 32),)),
        "latent_weight": scatter_about(key_of[3], (FF_W, D_W), FF_W ** -0.5, 0.0546875, ((0, 4), (1, 8))),
        "step_size": draw_step_size(jax.random.fold_in(key_of[5], 71), 0),
    }


top_level = 7.0
wobble = 0.9
two_pi = 6.283185307179586
inv_root_two = 0.7071067811865476
inv_root_tau = 0.3989422804014327


def gelu_pair(values):
    normal_cdf = 0.5 * (1.0 + jax.scipy.special.erf(values * inv_root_two))
    density = jnp.exp(-0.5 * values * values) * inv_root_tau
    return values * normal_cdf, normal_cdf + values * density


def soft_quantize(weight, step):
    ratio = weight / step
    clipped = top_level * jnp.tanh(ratio / top_level)
    phase = two_pi * clipped
    quantized = clipped - wobble * jnp.sin(phase) / two_pi
    slope = (1.0 - wobble * jnp.cos(phase)) * (1.0 - (clipped / top_level) * (clipped / top_level))
    return quantized, slope, ratio


def reference(patch_acts, patch_slot, out_grads, latent_weight, step_size):
    group_slots = patch_slot.reshape(N_FSDP, N_DP * PATCH_CAP).astype(jnp.int32)
    offsets = (jnp.arange(N_FSDP, dtype=jnp.int32) * (ROWS + 1))[:, None]
    target = (offsets + group_slots).reshape(-1).astype(jnp.int32)
    holder = jnp.zeros((N_FSDP * (ROWS + 1), FF_W), jnp.bfloat16).at[target].set(patch_acts)
    packed = holder.reshape(N_FSDP, ROWS + 1, FF_W)[:, :ROWS].reshape(N_FSDP * ROWS, FF_W)
    act_full, gelu_slope = gelu_pair(packed.astype(jnp.float32))
    act = act_full.astype(jnp.bfloat16)
    step_full = step_size.astype(jnp.float32)
    quantized, slope, ratio = soft_quantize(latent_weight.astype(jnp.float32), step_full)
    qweight = (step_full * quantized).astype(jnp.bfloat16)
    grad_hidden = jnp.dot(out_grads, qweight.T, preferred_element_type=jnp.float32)
    grad_packed = (grad_hidden * gelu_slope).astype(jnp.bfloat16)
    padded = jnp.concatenate([grad_packed.reshape(N_FSDP, ROWS, FF_W), jnp.zeros((N_FSDP, 1, FF_W), jnp.bfloat16)], axis=1)
    grad_acts = padded.reshape(N_FSDP * (ROWS + 1), FF_W)[target]
    grad_qweight = jnp.dot(act.T, out_grads, preferred_element_type=jnp.float32)
    grad_weight = grad_qweight * slope
    scale_factor = (FF_W * top_level) ** -0.5
    grad_step = scale_factor * jnp.sum(grad_qweight * (quantized - ratio * slope), axis=0, keepdims=True)
    return grad_acts, grad_weight, grad_step
```

```python
import jax
import jax.numpy as jnp
from jax import lax
from jax.sharding import PartitionSpec as P

FF_W = 12288


top_level = 7.0
wobble = 0.9
two_pi = 6.283185307179586
inv_root_two = 0.7071067811865476
inv_root_tau = 0.3989422804014327


def gelu_pair(values):
    normal_cdf = 0.5 * (1.0 + jax.scipy.special.erf(values * inv_root_two))
    density = jnp.exp(-0.5 * values * values) * inv_root_tau
    return (values * normal_cdf, normal_cdf + values * density)


def soft_quantize(weight, step):
    ratio = weight / step
    clipped = top_level * jnp.tanh(ratio / top_level)
    phase = two_pi * clipped
    quantized = clipped - wobble * jnp.sin(phase) / two_pi
    slope = (1.0 - wobble * jnp.cos(phase)) * (1.0 - clipped / top_level * (clipped / top_level))
    return (quantized, slope, ratio)


def contract(left, right, dims):
    return lax.dot_general(left, right, (dims, ((), ())), preferred_element_type=jnp.float32)


def shards(patch_acts, patch_slot, out_grads, latent_weight, step_size):
    dp_count = lax.axis_size("dp")
    fsdp_count = lax.axis_size("fsdp")
    line_count = fsdp_count // 2
    lines = [[2 * i + s for i in range(line_count)] for s in range(2)]
    swap = [(i, i ^ 1) for i in range(fsdp_count)]
    side = lax.rem(lax.axis_index("fsdp"), 2)
    capacity, features = patch_acts.shape
    hidden = features // dp_count
    own_rows, width = out_grads.shape
    packed_rows = own_rows * dp_count
    columns = width // fsdp_count

    grads = lax.all_to_all(
        out_grads.reshape(own_rows, line_count, 2 * columns), "fsdp",
        split_axis=1, concat_axis=0, tiled=True, axis_index_groups=lines,
    ).reshape(line_count * own_rows, 2 * columns)
    grads = lax.all_gather(grads, "dp", axis=0, tiled=False)
    grads = grads.reshape(dp_count, line_count, own_rows, 2 * columns).transpose(1, 0, 2, 3)
    grads = grads.reshape(line_count * packed_rows, 2 * columns)
    grads_own = lax.dynamic_slice_in_dim(grads, side * columns, columns, 1)
    grads_other = lax.dynamic_slice_in_dim(grads, (1 - side) * columns, columns, 1)

    outgoing = patch_acts.reshape(capacity, dp_count, hidden)
    incoming = lax.all_to_all(outgoing, "dp", split_axis=1, concat_axis=0, tiled=True)
    incoming = incoming.reshape(dp_count * capacity, hidden)
    slots = lax.all_gather(patch_slot, "dp", axis=0, tiled=True)
    place = (lax.broadcasted_iota(jnp.int32, (packed_rows, dp_count * capacity), 0) == slots[None, :])
    place = place.astype(jnp.bfloat16)

    step = step_size.astype(jnp.float32)
    quantized, slope, ratio = soft_quantize(latent_weight.astype(jnp.float32), step)
    weight_own = (step * quantized).astype(jnp.bfloat16)
    weight_other = lax.ppermute(weight_own, "fsdp", swap)

    packed = contract(place, incoming, ((1,), (0,)))
    act_full, gelu_slope = gelu_pair(packed)
    act = act_full.astype(jnp.bfloat16)

    partial_hidden = contract(grads_own, weight_own, ((1,), (1,))) + contract(
        grads_other, weight_other, ((1,), (1,))
    )
    grad_hidden = lax.psum_scatter(
        partial_hidden.astype(jnp.bfloat16), "fsdp",
        scatter_dimension=0, tiled=True, axis_index_groups=lines,
    ).astype(jnp.float32)
    act_all = lax.all_gather(act, "fsdp", axis=0, tiled=True, axis_index_groups=lines)

    grad_packed = (grad_hidden * gelu_slope).astype(jnp.bfloat16)
    picked = contract(place, grad_packed, ((0,), (0,))).astype(jnp.bfloat16)
    returned = lax.all_to_all(
        picked.reshape(dp_count * capacity, 1, hidden), "dp", split_axis=0, concat_axis=1, tiled=True
    )
    grad_acts = returned.reshape(capacity, features)

    half_other = contract(act_all, grads_other, ((0,), (0,))).astype(jnp.bfloat16)
    half_arrived = lax.ppermute(half_other, "fsdp", swap).astype(jnp.float32)
    grad_qweight = contract(act_all, grads_own, ((0,), (0,))) + half_arrived
    grad_weight = grad_qweight * slope
    partial_step = jnp.sum(grad_qweight * (quantized - ratio * slope), axis=0, keepdims=True)
    scale_factor = (FF_W * top_level) ** (-0.5)
    grad_step = scale_factor * lax.psum(partial_step, "dp")
    return (grad_acts, grad_weight, grad_step)


def solution(mesh):
    return jax.shard_map(
        shards,
        mesh=mesh,
        in_specs=(
            P(("fsdp", "dp"), None),
            P(("fsdp", "dp")),
            P(("fsdp", "dp"), None),
            P("dp", "fsdp"),
            P(None, "fsdp"),
        ),
        out_specs=(P(("fsdp", "dp"), None), P("dp", "fsdp"), P(None, "fsdp")),
        check_vma=False,
    )
```

```python
import functools

import jax
import jax.numpy as jnp
from jax import lax
from jax.experimental import pallas as pl
from jax.experimental.pallas import tpu as pltpu
from jax.sharding import PartitionSpec as P

FF_W = 12288
CHUNKS = 6
LAG = 1
MESH = pl.DeviceIdType.MESH

top_level = 7.0
wobble = 0.9
two_pi = 6.283185307179586
pi = 3.141592653589793
inv_root_two = 0.7071067811865476
inv_root_tau = 0.3989422804014327


def gelu_pair(values):
    normal_cdf = 0.5 * (1.0 + lax.erf(values * inv_root_two))
    density = jnp.exp(-0.5 * values * values) * inv_root_tau
    return (values * normal_cdf, normal_cdf + values * density)


def sin_cos_turns(turns):
    angle = pi * (turns - jnp.floor(turns + 0.5))
    square = angle * angle
    s = -1.0 / 39916800.0
    for c in (1.0 / 362880.0, -1.0 / 5040.0, 1.0 / 120.0, -1.0 / 6.0, 1.0):
        s = s * square + c
    s = s * angle
    c = 1.0 / 479001600.0
    for k in (-1.0 / 3628800.0, 1.0 / 40320.0, -1.0 / 720.0, 1.0 / 24.0, -0.5, 1.0):
        c = c * square + k
    return 2.0 * s * c, 1.0 - 2.0 * s * s


def soft_quantize(weight, step, inv_step):
    ratio = weight * inv_step
    unit = jnp.tanh(ratio * (1.0 / top_level))
    clipped = top_level * unit
    sine, cosine = sin_cos_turns(clipped)
    quantized = clipped - (wobble / two_pi) * sine
    slope = (1.0 - wobble * cosine) * (1.0 - unit * unit)
    return (step * quantized, slope, quantized - ratio * slope)


def dot(left, right, left_dim, right_dim):
    return lax.dot_general(
        left, right, (((left_dim,), (right_dim,)), ((), ())), preferred_element_type=jnp.float32
    )


def kernel(
    line, dps, acts_hbm, slots_ref, og_ref, latent_ref, step_ref,
    ga_hbm, gw_hbm, gstep_ref,
    inc, slot_all, place, acts, gelu_slope, gz, qw, rr, sl, res, gs, gr, tmp, stp,
    slot_recv, slot_send, ogz_recv, ogz_send, ogd_recv, ogd_send, inc_recv, inc_send,
    qw_recv, qw_send, ag_recv, ag_send, rs_recv, rs_send, gr_recv, gr_send,
    ga_recv, ga_send, gw_sem, st_recv, st_send,
):
    K = inc.shape[0]
    cap, width = inc.shape[2], inc.shape[3]
    rows = acts.shape[2]
    own_rows, cols = og_ref.shape[2], og_ref.shape[3]
    hidden = K * width
    f = lax.axis_index("fsdp")
    d = lax.axis_index("dp")
    me = lax.div(f, 2)
    side = lax.rem(f, 2)
    other = 1 - side

    def at(z, s, e):
        return (z * 2 + s, e)

    partner = at(me, other, d)
    right = at(jnp.minimum(me + 1, line - 1), side, d)
    left = at(jnp.maximum(me - 1, 0), side, d)
    mates = [lax.rem(d + j, dps) for j in range(1, dps)]
    others = [lax.rem(me + j, line) for j in range(1, line)]

    def remote(src, dst, send, recv, device):
        return pltpu.make_async_remote_copy(
            src_ref=src, dst_ref=dst, send_sem=send, recv_sem=recv,
            device_id=device, device_id_type=MESH,
        )

    def await_bytes(ref, sem):
        pltpu.make_async_copy(ref, ref, sem).wait()

    barrier = pltpu.get_barrier_semaphore()
    for z in others:
        pl.semaphore_signal(barrier, inc=1, device_id=at(z, side, d), device_id_type=MESH)
    for e in mates:
        pl.semaphore_signal(barrier, inc=1, device_id=at(me, side, e), device_id_type=MESH)
    pl.semaphore_signal(barrier, inc=1, device_id=partner, device_id_type=MESH)
    pl.semaphore_wait(barrier, line + dps - 1)

    for z in others:
        remote(og_ref.at[z], gz.at[:, me, d], ogz_send, ogz_recv.at[me], at(z, side, d)).start()
    for e in mates:
        remote(slots_ref, slot_all.at[d], slot_send, slot_recv, at(me, side, e)).start()
    slot_all[d] = slots_ref[...]
    gz[:, me, d] = og_ref[me]

    def send_acts(k):
        for e in mates:
            src = acts_hbm.at[:, pl.ds(pl.multiple_of(e * hidden + k * width, 128), width)]
            remote(src, inc.at[k, d], inc_send, inc_recv.at[k], at(me, side, e)).start()
        src = acts_hbm.at[:, pl.ds(pl.multiple_of(d * hidden + k * width, 128), width)]
        pltpu.make_async_copy(src, inc.at[k, d], inc_recv.at[k]).start()

    def forward_grads(z):
        for e in mates:
            remote(gz.at[:, z, d], gz.at[:, z, d], ogd_send, ogd_recv.at[z], at(me, side, e)).start()

    step = step_ref[...].astype(jnp.float32)
    inv_step = 1.0 / step

    def quantize(k):
        block = 16

        def body(i, carry):
            part = pl.ds(pl.multiple_of(i * block, block), block)
            weight = latent_ref[k, part, :].astype(jnp.float32)
            q, slope, rest = soft_quantize(weight, step, inv_step)
            qw[side, k, part, :] = q.astype(jnp.bfloat16)
            sl[k, part, :] = slope
            res[k, part, :] = rest
            return carry

        lax.fori_loop(0, width // block, body, 0)
        remote(qw.at[side, k], qw.at[side, k], qw_send, qw_recv.at[k], partner).start()

    send_acts(0)
    forward_grads(me)
    send_acts(1)
    quantize(0)

    @pl.when((me == 0) | (me == line - 1))
    def _():
        def body(k, carry):
            @pl.when(me == 0)
            def _():
                for z in range(line):
                    rr[k, z] = jnp.zeros((rows, width), jnp.bfloat16)

            @pl.when(me == line - 1)
            def _():
                for z in range(line - 1):
                    rr[k, z] = jnp.zeros((rows, width), jnp.bfloat16)
                rr[k, line] = jnp.zeros((rows, width), jnp.bfloat16)

            return carry

        lax.fori_loop(0, K, body, 0)

    for z in others:
        await_bytes(gz.at[:, z, d], ogz_recv.at[z])
        forward_grads(z)
    quantize(1)
    await_bytes(slot_all.at[pl.ds(0, dps - 1)], slot_recv)
    for e in range(dps):
        place[:, e * cap:(e + 1) * cap] = (
            lax.broadcasted_iota(jnp.int32, (rows, cap), 0) == slot_all[e]
        ).astype(jnp.float32).astype(jnp.bfloat16)
    stp[d] = jnp.zeros((1, cols), jnp.float32)

    def grads_of(s, z):
        return gz[s, z].reshape(rows, cols)

    def partial_hidden(z, k):
        return dot(grads_of(0, z), qw[0, k], 1, 1) + dot(grads_of(1, z), qw[1, k], 1, 1)

    def pack(k):
        await_bytes(inc.at[k], inc_recv.at[k])
        tmp[...] = dot(place[...], inc[k].reshape(dps * cap, width), 1, 0)
        block = 16

        def body(i, carry):
            part = pl.ds(pl.multiple_of(i * block, block), block)
            act, slope = gelu_pair(tmp[part, :])
            acts[k, me, part, :] = act.astype(jnp.bfloat16)
            gelu_slope[k, part, :] = slope
            return carry

        lax.fori_loop(0, rows // block, body, 0)
        send_line(k, me, True, True)

    def send_line(k, z, to_right, to_left):
        block = acts.at[k, z]
        if to_right:
            @pl.when(me < line - 1)
            def _():
                remote(block, block, ag_send, ag_recv.at[k, z], right).start()
        if to_left:
            @pl.when(me > 0)
            def _():
                remote(block, block, ag_send, ag_recv.at[k, z], left).start()

    def hop(k, h):
        @pl.when(me - h >= 0)
        def _():
            z = me - h
            await_bytes(acts.at[k, z], ag_recv.at[k, z])
            send_line(k, z, True, False)

        @pl.when(me + h <= line - 1)
        def _():
            z = me + h
            await_bytes(acts.at[k, z], ag_recv.at[k, z])
            send_line(k, z, False, True)

    def sum_right(k):
        for j in range(line - 1, 0, -1):
            @pl.when(me + j <= line - 1)
            def _():
                z = me + j

                @pl.when(me > 0)
                def _():
                    await_bytes(rr.at[k, z], rs_recv.at[k, z])

                total = rr[k, z].astype(jnp.float32) + partial_hidden(z, k)
                rr[k, z] = total.astype(jnp.bfloat16)
                remote(rr.at[k, z], rr.at[k, z], rs_send, rs_recv.at[k, z], right).start()

    def sum_left(k):
        for j in range(line - 1, 0, -1):
            @pl.when(me - j >= 0)
            def _():
                z = me - j
                slot = line if j == 1 else z

                @pl.when(me < line - 1)
                def _():
                    await_bytes(rr.at[k, z], rs_recv.at[k, z])

                total = rr[k, z].astype(jnp.float32) + partial_hidden(z, k)
                rr[k, z] = total.astype(jnp.bfloat16)
                remote(rr.at[k, z], rr.at[k, slot], rs_send, rs_recv.at[k, slot], left).start()

    def finish_hidden(k):
        @pl.when(me > 0)
        def _():
            await_bytes(rr.at[k, me], rs_recv.at[k, me])

        @pl.when(me < line - 1)
        def _():
            await_bytes(rr.at[k, line], rs_recv.at[k, line])

        total = rr[k, me].astype(jnp.float32) + rr[k, line].astype(jnp.float32) + partial_hidden(me, k)
        packed = (total * gelu_slope[k]).astype(jnp.bfloat16)
        picked = dot(place[...], packed, 0, 0).astype(jnp.bfloat16)
        inc[k] = picked.reshape(dps, cap, width)
        here = ga_hbm.at[:, pl.ds(pl.multiple_of(d * hidden + k * width, 128), width)]
        for e in mates:
            remote(inc.at[k, e], here, ga_send, ga_recv, at(me, side, e)).start()
        pltpu.make_async_copy(inc.at[k, d], here, ga_recv).start()

    def weight_half(k, s):
        return dot(acts[k].reshape(line * rows, width), gz[s].reshape(line * rows, cols), 0, 0)

    def send_half(k):
        gs[k] = weight_half(k, other).astype(jnp.bfloat16)
        remote(gs.at[k], gr.at[k], gr_send, gr_recv.at[k], partner).start()

    def finish_weight(k):
        own = weight_half(k, side)
        await_bytes(gr.at[k], gr_recv.at[k])
        total = own + gr[k].astype(jnp.float32)
        stp[d] += jnp.sum(total * res[k], axis=0, keepdims=True)
        sl[k] = total * sl[k]
        pltpu.make_async_copy(
            sl.at[k], gw_hbm.at[pl.ds(pl.multiple_of(k * width, 16), width), :], gw_sem
        ).start()

    def when_chunk(k, act):
        @pl.when((k >= 0) & (k < K))
        def _():
            act(k)

    def await_grads():
        for z in range(line):
            await_bytes(gz.at[:, z, pl.ds(0, dps - 1)], ogd_recv.at[z])

    depth = LAG * (line - 1)

    def turn(t, carry):
        when_chunk(t, pack)

        @pl.when(t == 0)
        def _():
            await_grads()

        when_chunk(t, lambda k: await_bytes(qw.at[other, k], qw_recv.at[k]))
        for h in range(1, line):
            when_chunk(t - LAG * h, lambda k, h=h: hop(k, h))
        when_chunk(t - LAG * me, sum_right)
        when_chunk(t - LAG * (line - 1 - me), sum_left)

        @pl.when(t + 2 < K)
        def _():
            send_acts(t + 2)
            quantize(t + 2)

        when_chunk(t - depth, finish_hidden)
        when_chunk(t - depth, send_half)
        when_chunk(t - depth - LAG, finish_weight)
        return carry

    lax.fori_loop(0, K + depth + LAG, turn, 0)

    for e in mates:
        remote(stp.at[d], stp.at[d], st_send, st_recv, at(me, side, e)).start()
    await_bytes(stp.at[pl.ds(0, dps - 1)], st_recv)
    total = stp[0]
    for e in range(1, dps):
        total = total + stp[e]
    gstep_ref[...] = ((FF_W * top_level) ** (-0.5)) * total

    await_bytes(stp.at[pl.ds(0, dps - 1)], st_send)
    await_bytes(slot_all.at[pl.ds(0, dps - 1)], slot_send)
    await_bytes(gz.at[:, pl.ds(0, line - 1), 0], ogz_send)
    await_bytes(gz.at[:, :, pl.ds(0, dps - 1)], ogd_send)
    await_bytes(inc.at[:, pl.ds(0, dps - 1)], inc_send)
    await_bytes(qw.at[0], qw_send)
    await_bytes(gs, gr_send)
    await_bytes(rr.at[:, pl.ds(0, line - 1)], rs_send)

    @pl.when((me == 0) | (me == line - 1))
    def _():
        await_bytes(acts.at[:, 0], ag_send)

    @pl.when((me > 0) & (me < line - 1))
    def _():
        await_bytes(rr, ag_send)

    await_bytes(inc.at[:, pl.ds(0, dps - 1)], ga_send)
    await_bytes(inc, ga_recv)
    await_bytes(sl, gw_sem)


def shards(patch_acts, patch_slot, out_grads, latent_weight, step_size):
    dps = lax.axis_size("dp")
    line = lax.axis_size("fsdp") // 2
    cap, features = patch_acts.shape
    hidden = features // dps
    own_rows, all_columns = out_grads.shape
    rows = own_rows * dps
    cols = latent_weight.shape[1]
    K = CHUNKS
    width = hidden // K
    grads = out_grads.reshape(own_rows, line, 2, cols).transpose(1, 2, 0, 3)
    bf16, f32 = jnp.bfloat16, jnp.float32
    vmem = pl.BlockSpec(memory_space=pltpu.VMEM)
    hbm = pl.BlockSpec(memory_space=pl.ANY)
    dma = pltpu.SemaphoreType.DMA
    return pl.pallas_call(
        functools.partial(kernel, line, dps),
        out_shape=(
            jax.ShapeDtypeStruct((cap, features), bf16),
            jax.ShapeDtypeStruct((hidden, cols), f32),
            jax.ShapeDtypeStruct((1, cols), f32),
        ),
        in_specs=[hbm, vmem, vmem, vmem, vmem],
        out_specs=(hbm, hbm, vmem),
        scratch_shapes=[
            pltpu.VMEM((K, dps, cap, width), bf16),
            pltpu.VMEM((dps, 1, cap), jnp.int32),
            pltpu.VMEM((rows, dps * cap), bf16),
            pltpu.VMEM((K, line, rows, width), bf16),
            pltpu.VMEM((K, rows, width), f32),
            pltpu.VMEM((2, line, dps, own_rows, cols), bf16),
            pltpu.VMEM((2, K, width, cols), bf16),
            pltpu.VMEM((K, line + 1, rows, width), bf16),
            pltpu.VMEM((K, width, cols), f32),
            pltpu.VMEM((K, width, cols), f32),
            pltpu.VMEM((K, width, cols), bf16),
            pltpu.VMEM((K, width, cols), bf16),
            pltpu.VMEM((rows, width), f32),
            pltpu.VMEM((dps, 1, cols), f32),
            dma, dma, dma((line,)), dma, dma((line,)), dma, dma((K,)), dma,
            dma((K,)), dma, dma((K, line)), dma, dma((K, line + 1)), dma, dma((K,)), dma,
            dma, dma, dma, dma, dma,
        ],
        compiler_params=pltpu.CompilerParams(
            collective_id=0, has_side_effects=True, vmem_limit_bytes=60 * 1024 * 1024
        ),
        cost_estimate=pl.CostEstimate(
            flops=8 * line * rows * hidden * cols, bytes_accessed=4 * cap * features,
            transcendentals=0,
        ),
    )(patch_acts, patch_slot.reshape(1, cap), grads, latent_weight.reshape(K, width, cols), step_size)


def solution(mesh):
    return jax.shard_map(
        shards,
        mesh=mesh,
        in_specs=(
            P(("fsdp", "dp"), None),
            P(("fsdp", "dp")),
            P(("fsdp", "dp"), None),
            P("dp", "fsdp"),
            P(None, "fsdp"),
        ),
        out_specs=(P(("fsdp", "dp"), None), P("dp", "fsdp"), P(None, "fsdp")),
        check_vma=False,
    )
```

```python
import functools

import jax
import jax.numpy as jnp
from jax import lax
from jax.experimental import pallas as pl
from jax.experimental.pallas import tpu as pltpu
from jax.sharding import PartitionSpec as P

FF_W = 12288
CHUNKS = 12
LAG = 2
BEHIND = 2
AHEAD = 4
MESH = pl.DeviceIdType.MESH

top_level = 7.0
wobble = 0.9
two_pi = 6.283185307179586
pi = 3.141592653589793
inv_root_two = 0.7071067811865476
inv_root_tau = 0.3989422804014327


def gelu_pair(values):
    normal_cdf = 0.5 * (1.0 + lax.erf(values * inv_root_two))
    density = jnp.exp(-0.5 * values * values) * inv_root_tau
    return (values * normal_cdf, normal_cdf + values * density)


def sin_cos_turns(turns):
    angle = pi * (turns - jnp.floor(turns + 0.5))
    square = angle * angle
    s = -1.0 / 39916800.0
    for c in (1.0 / 362880.0, -1.0 / 5040.0, 1.0 / 120.0, -1.0 / 6.0, 1.0):
        s = s * square + c
    s = s * angle
    c = 1.0 / 479001600.0
    for k in (-1.0 / 3628800.0, 1.0 / 40320.0, -1.0 / 720.0, 1.0 / 24.0, -0.5, 1.0):
        c = c * square + k
    return 2.0 * s * c, 1.0 - 2.0 * s * s


def soft_quantize(weight, step, inv_step):
    ratio = weight * inv_step
    unit = jnp.tanh(ratio * (1.0 / top_level))
    clipped = top_level * unit
    sine, cosine = sin_cos_turns(clipped)
    quantized = clipped - (wobble / two_pi) * sine
    slope = (1.0 - wobble * cosine) * (1.0 - unit * unit)
    return (step * quantized, slope, quantized - ratio * slope)


def dot(left, right, left_dim, right_dim):
    return lax.dot_general(
        left, right, (((left_dim,), (right_dim,)), ((), ())), preferred_element_type=jnp.float32
    )


def kernel(
    line, dps, acts_hbm, slots_ref, og_ref, latent_ref, step_ref,
    ga_hbm, gw_hbm, gstep_ref,
    inc, slot_all, place, acts, gelu_slope, gz, qw, rr, sl, res, gs, gr, tmp, stp,
    slot_recv, slot_send, ogz_recv, ogz_send, ogd_recv, ogd_send, inc_recv, inc_send,
    qw_recv, qw_send, ag_recv, ag_send, rs_recv, rs_send, gr_recv, gr_send,
    ga_recv, ga_send, gw_sem, st_recv, st_send,
):
    K = inc.shape[0]
    cap, width = inc.shape[2], inc.shape[3]
    rows = acts.shape[2]
    own_rows, cols = og_ref.shape[2], og_ref.shape[3]
    hidden = K * width
    f = lax.axis_index("fsdp")
    d = lax.axis_index("dp")
    me = lax.div(f, 2)
    side = lax.rem(f, 2)
    other = 1 - side

    def at(z, s, e):
        return (z * 2 + s, e)

    partner = at(me, other, d)
    right = at(jnp.minimum(me + 1, line - 1), side, d)
    left = at(jnp.maximum(me - 1, 0), side, d)
    mates = [lax.rem(d + j, dps) for j in range(1, dps)]
    others = [lax.rem(me + j, line) for j in range(1, line)]

    def remote(src, dst, send, recv, device):
        return pltpu.make_async_remote_copy(
            src_ref=src, dst_ref=dst, send_sem=send, recv_sem=recv,
            device_id=device, device_id_type=MESH,
        )

    def await_bytes(ref, sem):
        pltpu.make_async_copy(ref, ref, sem).wait()

    barrier = pltpu.get_barrier_semaphore()
    for z in others:
        pl.semaphore_signal(barrier, inc=1, device_id=at(z, side, d), device_id_type=MESH)
    for e in mates:
        pl.semaphore_signal(barrier, inc=1, device_id=at(me, side, e), device_id_type=MESH)
    pl.semaphore_signal(barrier, inc=1, device_id=partner, device_id_type=MESH)
    pl.semaphore_wait(barrier, line + dps - 1)

    for z in others:
        remote(og_ref.at[z], gz.at[:, me, d], ogz_send, ogz_recv.at[me], at(z, side, d)).start()
    for e in mates:
        remote(slots_ref, slot_all.at[d], slot_send, slot_recv, at(me, side, e)).start()
    slot_all[d] = slots_ref[...]
    gz[:, me, d] = og_ref[me]

    def send_acts(k):
        for e in mates:
            src = acts_hbm.at[:, pl.ds(pl.multiple_of(e * hidden + k * width, 128), width)]
            remote(src, inc.at[k, d], inc_send, inc_recv.at[k], at(me, side, e)).start()
        src = acts_hbm.at[:, pl.ds(pl.multiple_of(d * hidden + k * width, 128), width)]
        pltpu.make_async_copy(src, inc.at[k, d], inc_recv.at[k]).start()

    def forward_grads(z):
        for e in mates:
            remote(gz.at[:, z, d], gz.at[:, z, d], ogd_send, ogd_recv.at[z], at(me, side, e)).start()

    step = step_ref[...].astype(jnp.float32)
    inv_step = 1.0 / step

    def quantize(k):
        block = 32

        def body(i, carry):
            part = pl.ds(pl.multiple_of(i * block, block), block)
            weight = latent_ref[k, part, :].astype(jnp.float32)
            q, slope, rest = soft_quantize(weight, step, inv_step)
            qw[side, k, part, :] = q.astype(jnp.bfloat16)
            sl[k, part, :] = slope
            res[k, part, :] = rest
            return carry

        lax.fori_loop(0, width // block, body, 0)
        remote(qw.at[side, k], qw.at[side, k], qw_send, qw_recv.at[k], partner).start()

    for k in range(min(AHEAD, K)):
        send_acts(k)
        if k == 0:
            forward_grads(me)
    stp[d] = jnp.zeros((1, cols), jnp.float32)
    quantize(0)
    await_bytes(slot_all.at[pl.ds(0, dps - 1)], slot_recv)
    for e in range(dps):
        place[:, e * cap:(e + 1) * cap] = (
            lax.broadcasted_iota(jnp.int32, (rows, cap), 0) == slot_all[e]
        ).astype(jnp.float32).astype(jnp.bfloat16)

    def clear(k, slot):
        rr[k, slot] = jnp.zeros((rows, width), jnp.bfloat16)

    def grads_of(s, z):
        return gz[s, z].reshape(rows, cols)

    def partial_hidden(z, k):
        return dot(grads_of(0, z), qw[0, k], 1, 1) + dot(grads_of(1, z), qw[1, k], 1, 1)

    def pack(k):
        await_bytes(inc.at[k], inc_recv.at[k])
        tmp[...] = dot(place[...], inc[k].reshape(dps * cap, width), 1, 0)
        block = 32

        def body(i, carry):
            part = pl.ds(pl.multiple_of(i * block, block), block)
            act, slope = gelu_pair(tmp[part, :])
            acts[k, me, part, :] = act.astype(jnp.bfloat16)
            gelu_slope[k, part, :] = slope
            return carry

        lax.fori_loop(0, rows // block, body, 0)
        send_line(k, me, True, True)

    def send_line(k, z, to_right, to_left):
        block = acts.at[k, z]
        if to_right:
            @pl.when(me < line - 1)
            def _():
                remote(block, block, ag_send, ag_recv.at[k, z], right).start()
        if to_left:
            @pl.when(me > 0)
            def _():
                remote(block, block, ag_send, ag_recv.at[k, z], left).start()

    def hop(k, h):
        @pl.when(me - h >= 0)
        def _():
            z = me - h
            await_bytes(acts.at[k, z], ag_recv.at[k, z])
            send_line(k, z, True, False)

        @pl.when(me + h <= line - 1)
        def _():
            z = me + h
            await_bytes(acts.at[k, z], ag_recv.at[k, z])
            send_line(k, z, False, True)

    def sum_right(k):
        for j in range(line - 1, 0, -1):
            @pl.when(me + j <= line - 1)
            def _():
                z = me + j

                @pl.when(me > 0)
                def _():
                    await_bytes(rr.at[k, z], rs_recv.at[k, z])

                @pl.when(me == 0)
                def _():
                    clear(k, z)

                total = rr[k, z].astype(jnp.float32) + partial_hidden(z, k)
                rr[k, z] = total.astype(jnp.bfloat16)
                remote(rr.at[k, z], rr.at[k, z], rs_send, rs_recv.at[k, z], right).start()

    def sum_left(k):
        for j in range(line - 1, 0, -1):
            @pl.when(me - j >= 0)
            def _():
                z = me - j
                slot = line if j == 1 else z

                @pl.when(me < line - 1)
                def _():
                    await_bytes(rr.at[k, z], rs_recv.at[k, z])

                @pl.when(me == line - 1)
                def _():
                    clear(k, z)

                total = rr[k, z].astype(jnp.float32) + partial_hidden(z, k)
                rr[k, z] = total.astype(jnp.bfloat16)
                remote(rr.at[k, z], rr.at[k, slot], rs_send, rs_recv.at[k, slot], left).start()

    def finish_hidden(k):
        @pl.when(me > 0)
        def _():
            await_bytes(rr.at[k, me], rs_recv.at[k, me])

        @pl.when(me < line - 1)
        def _():
            await_bytes(rr.at[k, line], rs_recv.at[k, line])

        @pl.when(me == 0)
        def _():
            clear(k, me)

        @pl.when(me == line - 1)
        def _():
            clear(k, line)

        total = rr[k, me].astype(jnp.float32) + rr[k, line].astype(jnp.float32) + partial_hidden(me, k)
        packed = (total * gelu_slope[k]).astype(jnp.bfloat16)
        picked = dot(place[...], packed, 0, 0).astype(jnp.bfloat16)
        inc[k] = picked.reshape(dps, cap, width)
        here = ga_hbm.at[:, pl.ds(pl.multiple_of(d * hidden + k * width, 128), width)]
        for e in mates:
            remote(inc.at[k, e], here, ga_send, ga_recv, at(me, side, e)).start()
        pltpu.make_async_copy(inc.at[k, d], here, ga_recv).start()

    def weight_half(k, s):
        return dot(acts[k].reshape(line * rows, width), gz[s].reshape(line * rows, cols), 0, 0)

    def send_half(k):
        gs[k] = weight_half(k, other).astype(jnp.bfloat16)
        remote(gs.at[k], gr.at[k], gr_send, gr_recv.at[k], partner).start()

    def finish_weight(k):
        own = weight_half(k, side)
        await_bytes(gr.at[k], gr_recv.at[k])
        total = own + gr[k].astype(jnp.float32)
        stp[d] += jnp.sum(total * res[k], axis=0, keepdims=True)
        sl[k] = total * sl[k]
        pltpu.make_async_copy(
            sl.at[k], gw_hbm.at[pl.ds(pl.multiple_of(k * width, 16), width), :], gw_sem
        ).start()

    def when_chunk(k, act):
        @pl.when((k >= 0) & (k < K))
        def _():
            act(k)

    def await_grads():
        for z in range(line):
            await_bytes(gz.at[:, z, pl.ds(0, dps - 1)], ogd_recv.at[z])

    depth = LAG * (line - 1)

    def turn(t, carry):
        when_chunk(t, pack)

        @pl.when(t == 0)
        def _():
            for z in others:
                await_bytes(gz.at[:, z, d], ogz_recv.at[z])
                forward_grads(z)

        for h in range(1, line):
            when_chunk(t - LAG * h, lambda k, h=h: hop(k, h))

        @pl.when(t == BEHIND)
        def _():
            await_grads()

        when_chunk(t - BEHIND, lambda k: await_bytes(qw.at[other, k], qw_recv.at[k]))
        when_chunk(t - BEHIND - LAG * me, sum_right)
        when_chunk(t - BEHIND - LAG * (line - 1 - me), sum_left)

        @pl.when(t + AHEAD < K)
        def _():
            send_acts(t + AHEAD)

        @pl.when(t + 1 < K)
        def _():
            quantize(t + 1)

        when_chunk(t - BEHIND - depth, finish_hidden)
        when_chunk(t - depth, send_half)
        when_chunk(t - depth - LAG, finish_weight)
        return carry

    lax.fori_loop(0, K + depth + max(LAG, BEHIND), turn, 0)

    for e in mates:
        remote(stp.at[d], stp.at[d], st_send, st_recv, at(me, side, e)).start()
    await_bytes(stp.at[pl.ds(0, dps - 1)], st_recv)
    total = stp[0]
    for e in range(1, dps):
        total = total + stp[e]
    gstep_ref[...] = ((FF_W * top_level) ** (-0.5)) * total

    await_bytes(stp.at[pl.ds(0, dps - 1)], st_send)
    await_bytes(slot_all.at[pl.ds(0, dps - 1)], slot_send)
    await_bytes(gz.at[:, pl.ds(0, line - 1), 0], ogz_send)
    await_bytes(gz.at[:, :, pl.ds(0, dps - 1)], ogd_send)
    await_bytes(inc.at[:, pl.ds(0, dps - 1)], inc_send)
    await_bytes(qw.at[0], qw_send)
    await_bytes(gs, gr_send)
    await_bytes(rr.at[:, pl.ds(0, line - 1)], rs_send)

    @pl.when((me == 0) | (me == line - 1))
    def _():
        await_bytes(acts.at[:, 0], ag_send)

    @pl.when((me > 0) & (me < line - 1))
    def _():
        await_bytes(rr, ag_send)

    await_bytes(inc.at[:, pl.ds(0, dps - 1)], ga_send)
    await_bytes(inc, ga_recv)
    await_bytes(sl, gw_sem)


def shards(patch_acts, patch_slot, out_grads, latent_weight, step_size):
    dps = lax.axis_size("dp")
    line = lax.axis_size("fsdp") // 2
    cap, features = patch_acts.shape
    hidden = features // dps
    own_rows, all_columns = out_grads.shape
    rows = own_rows * dps
    cols = latent_weight.shape[1]
    K = min(CHUNKS, hidden // 128)
    width = hidden // K
    grads = out_grads.reshape(own_rows, line, 2, cols).transpose(1, 2, 0, 3)
    bf16, f32 = jnp.bfloat16, jnp.float32
    vmem = pl.BlockSpec(memory_space=pltpu.VMEM)
    hbm = pl.BlockSpec(memory_space=pl.ANY)
    dma = pltpu.SemaphoreType.DMA
    return pl.pallas_call(
        functools.partial(kernel, line, dps),
        out_shape=(
            jax.ShapeDtypeStruct((cap, features), bf16),
            jax.ShapeDtypeStruct((hidden, cols), f32),
            jax.ShapeDtypeStruct((1, cols), f32),
        ),
        in_specs=[hbm, vmem, vmem, vmem, vmem],
        out_specs=(hbm, hbm, vmem),
        scratch_shapes=[
            pltpu.VMEM((K, dps, cap, width), bf16),
            pltpu.VMEM((dps, 1, cap), jnp.int32),
            pltpu.VMEM((rows, dps * cap), bf16),
            pltpu.VMEM((K, line, rows, width), bf16),
            pltpu.VMEM((K, rows, width), f32),
            pltpu.VMEM((2, line, dps, own_rows, cols), bf16),
            pltpu.VMEM((2, K, width, cols), bf16),
            pltpu.VMEM((K, line + 1, rows, width), bf16),
            pltpu.VMEM((K, width, cols), f32),
            pltpu.VMEM((K, width, cols), f32),
            pltpu.VMEM((K, width, cols), bf16),
            pltpu.VMEM((K, width, cols), bf16),
            pltpu.VMEM((rows, width), f32),
            pltpu.VMEM((dps, 1, cols), f32),
            dma, dma, dma((line,)), dma, dma((line,)), dma, dma((K,)), dma,
            dma((K,)), dma, dma((K, line)), dma, dma((K, line + 1)), dma, dma((K,)), dma,
            dma, dma, dma, dma, dma,
        ],
        compiler_params=pltpu.CompilerParams(
            collective_id=0, has_side_effects=True, vmem_limit_bytes=60 * 1024 * 1024
        ),
        cost_estimate=pl.CostEstimate(
            flops=8 * line * rows * hidden * cols, bytes_accessed=4 * cap * features,
            transcendentals=0,
        ),
    )(patch_acts, patch_slot.reshape(1, cap), grads, latent_weight.reshape(K, width, cols), step_size)


def solution(mesh):
    return jax.shard_map(
        shards,
        mesh=mesh,
        in_specs=(
            P(("fsdp", "dp"), None),
            P(("fsdp", "dp")),
            P(("fsdp", "dp"), None),
            P("dp", "fsdp"),
            P(None, "fsdp"),
        ),
        out_specs=(P(("fsdp", "dp"), None), P("dp", "fsdp"), P(None, "fsdp")),
        check_vma=False,
    )
```

```python
import functools

import jax
import jax.numpy as jnp
from jax import lax
from jax.experimental import pallas as pl
from jax.experimental.pallas import tpu as pltpu
from jax.sharding import PartitionSpec as P

FF_W = 12288
CHUNKS = 12
LAG = 2
BEHIND = 4
AHEAD = 4
MESH = pl.DeviceIdType.MESH

top_level = 7.0
wobble = 0.9
two_pi = 6.283185307179586
pi = 3.141592653589793
inv_root_two = 0.7071067811865476
inv_root_tau = 0.3989422804014327


def gelu_pair(values):
    normal_cdf = 0.5 * (1.0 + lax.erf(values * inv_root_two))
    density = jnp.exp(-0.5 * values * values) * inv_root_tau
    return (values * normal_cdf, normal_cdf + values * density)


def sin_cos_turns(turns):
    angle = pi * (turns - jnp.floor(turns + 0.5))
    square = angle * angle
    s = -1.0 / 39916800.0
    for c in (1.0 / 362880.0, -1.0 / 5040.0, 1.0 / 120.0, -1.0 / 6.0, 1.0):
        s = s * square + c
    s = s * angle
    c = 1.0 / 479001600.0
    for k in (-1.0 / 3628800.0, 1.0 / 40320.0, -1.0 / 720.0, 1.0 / 24.0, -0.5, 1.0):
        c = c * square + k
    return 2.0 * s * c, 1.0 - 2.0 * s * s


def soft_quantize(weight, step, inv_step):
    ratio = weight * inv_step
    unit = jnp.tanh(ratio * (1.0 / top_level))
    clipped = top_level * unit
    sine, cosine = sin_cos_turns(clipped)
    quantized = clipped - (wobble / two_pi) * sine
    slope = (1.0 - wobble * cosine) * (1.0 - unit * unit)
    return (step * quantized, slope, quantized - ratio * slope)


def dot(left, right, left_dim, right_dim):
    return lax.dot_general(
        left, right, (((left_dim,), (right_dim,)), ((), ())), preferred_element_type=jnp.float32
    )


def kernel(
    line, dps, acts_hbm, slots_ref, og_ref, latent_ref, step_ref,
    ga_hbm, gw_hbm, gstep_ref,
    inc, slot_all, place, acts, gelu_slope, gz, qw, rr, sl, res, gs, gr, tmp, stp,
    slot_recv, slot_send, ogz_recv, ogz_send, ogd_recv, ogd_send, inc_recv, inc_send,
    qw_recv, qw_send, ag_recv, ag_send, rs_recv, rs_send, gr_recv, gr_send,
    ga_recv, ga_send, gw_sem, st_recv, st_send,
):
    K = inc.shape[0]
    cap, width = inc.shape[2], inc.shape[3]
    rows = acts.shape[2]
    own_rows, cols = og_ref.shape[2], og_ref.shape[3]
    hidden = K * width
    f = lax.axis_index("fsdp")
    d = lax.axis_index("dp")
    me = lax.div(f, 2)
    side = lax.rem(f, 2)
    other = 1 - side

    def at(z, s, e):
        return (z * 2 + s, e)

    partner = at(me, other, d)
    right = at(jnp.minimum(me + 1, line - 1), side, d)
    left = at(jnp.maximum(me - 1, 0), side, d)
    mates = [lax.rem(d + j, dps) for j in range(1, dps)]
    others = [lax.rem(me + j, line) for j in range(1, line)]

    def remote(src, dst, send, recv, device):
        return pltpu.make_async_remote_copy(
            src_ref=src, dst_ref=dst, send_sem=send, recv_sem=recv,
            device_id=device, device_id_type=MESH,
        )

    def await_bytes(ref, sem):
        pltpu.make_async_copy(ref, ref, sem).wait()

    barrier = pltpu.get_barrier_semaphore()
    for z in others:
        pl.semaphore_signal(barrier, inc=1, device_id=at(z, side, d), device_id_type=MESH)
    for e in mates:
        pl.semaphore_signal(barrier, inc=1, device_id=at(me, side, e), device_id_type=MESH)
    pl.semaphore_signal(barrier, inc=1, device_id=partner, device_id_type=MESH)
    pl.semaphore_wait(barrier, line + dps - 1)

    for z in others:
        remote(og_ref.at[z], gz.at[:, me, d], ogz_send, ogz_recv.at[me], at(z, side, d)).start()
    for e in mates:
        remote(slots_ref, slot_all.at[d], slot_send, slot_recv, at(me, side, e)).start()
    slot_all[d] = slots_ref[...]
    gz[:, me, d] = og_ref[me]

    def send_acts(k):
        for e in mates:
            src = acts_hbm.at[:, pl.ds(pl.multiple_of(e * hidden + k * width, 128), width)]
            remote(src, inc.at[k, d], inc_send, inc_recv.at[k], at(me, side, e)).start()
        src = acts_hbm.at[:, pl.ds(pl.multiple_of(d * hidden + k * width, 128), width)]
        pltpu.make_async_copy(src, inc.at[k, d], inc_recv.at[k]).start()

    def forward_grads(z):
        for e in mates:
            remote(gz.at[:, z, d], gz.at[:, z, d], ogd_send, ogd_recv.at[z], at(me, side, e)).start()

    step = step_ref[...].astype(jnp.float32)
    inv_step = 1.0 / step

    def quantize(k):
        block = 32

        def body(i, carry):
            part = pl.ds(pl.multiple_of(i * block, block), block)
            weight = latent_ref[k, part, :].astype(jnp.float32)
            q, slope, rest = soft_quantize(weight, step, inv_step)
            qw[side, k, part, :] = q.astype(jnp.bfloat16)
            sl[k, part, :] = slope
            res[k, part, :] = rest
            return carry

        lax.fori_loop(0, width // block, body, 0)
        remote(qw.at[side, k], qw.at[side, k], qw_send, qw_recv.at[k], partner).start()

    send_acts(0)
    forward_grads(me)
    stp[d] = jnp.zeros((1, cols), jnp.float32)
    quantize(0)
    await_bytes(slot_all.at[pl.ds(0, dps - 1)], slot_recv)
    for e in range(dps):
        place[:, e * cap:(e + 1) * cap] = (
            lax.broadcasted_iota(jnp.int32, (rows, cap), 0) == slot_all[e]
        ).astype(jnp.float32).astype(jnp.bfloat16)
    send_acts(1)
    for z in others:
        await_bytes(gz.at[:, z, d], ogz_recv.at[z])
        forward_grads(z)
    for k in range(2, min(AHEAD, K)):
        send_acts(k)

    def clear(k, slot):
        rr[k, slot] = jnp.zeros((rows, width), jnp.bfloat16)

    def grads_of(s, z):
        return gz[s, z].reshape(rows, cols)

    def partial_hidden(z, k):
        return dot(grads_of(0, z), qw[0, k], 1, 1) + dot(grads_of(1, z), qw[1, k], 1, 1)

    def pack(k):
        await_bytes(inc.at[k], inc_recv.at[k])
        tmp[...] = dot(place[...], inc[k].reshape(dps * cap, width), 1, 0)
        block = 32

        def body(i, carry):
            part = pl.ds(pl.multiple_of(i * block, block), block)
            act, slope = gelu_pair(tmp[part, :])
            acts[k, me, part, :] = act.astype(jnp.bfloat16)
            gelu_slope[k, part, :] = slope
            return carry

        lax.fori_loop(0, rows // block, body, 0)
        send_line(k, me, True, True)

    def send_line(k, z, to_right, to_left):
        block = acts.at[k, z]
        if to_right:
            @pl.when(me < line - 1)
            def _():
                remote(block, block, ag_send, ag_recv.at[k, z], right).start()
        if to_left:
            @pl.when(me > 0)
            def _():
                remote(block, block, ag_send, ag_recv.at[k, z], left).start()

    def hop(k, h):
        @pl.when(me - h >= 0)
        def _():
            z = me - h
            await_bytes(acts.at[k, z], ag_recv.at[k, z])
            send_line(k, z, True, False)

        @pl.when(me + h <= line - 1)
        def _():
            z = me + h
            await_bytes(acts.at[k, z], ag_recv.at[k, z])
            send_line(k, z, False, True)

    def sum_right(k):
        for j in range(line - 1, 0, -1):
            @pl.when(me + j <= line - 1)
            def _():
                z = me + j

                @pl.when(me > 0)
                def _():
                    await_bytes(rr.at[k, z], rs_recv.at[k, z])

                @pl.when(me == 0)
                def _():
                    clear(k, z)

                total = rr[k, z].astype(jnp.float32) + partial_hidden(z, k)
                rr[k, z] = total.astype(jnp.bfloat16)
                remote(rr.at[k, z], rr.at[k, z], rs_send, rs_recv.at[k, z], right).start()

    def sum_left(k):
        for j in range(line - 1, 0, -1):
            @pl.when(me - j >= 0)
            def _():
                z = me - j
                slot = line if j == 1 else z

                @pl.when(me < line - 1)
                def _():
                    await_bytes(rr.at[k, z], rs_recv.at[k, z])

                @pl.when(me == line - 1)
                def _():
                    clear(k, z)

                total = rr[k, z].astype(jnp.float32) + partial_hidden(z, k)
                rr[k, z] = total.astype(jnp.bfloat16)
                remote(rr.at[k, z], rr.at[k, slot], rs_send, rs_recv.at[k, slot], left).start()

    def finish_hidden(k):
        @pl.when(me > 0)
        def _():
            await_bytes(rr.at[k, me], rs_recv.at[k, me])

        @pl.when(me < line - 1)
        def _():
            await_bytes(rr.at[k, line], rs_recv.at[k, line])

        @pl.when(me == 0)
        def _():
            clear(k, me)

        @pl.when(me == line - 1)
        def _():
            clear(k, line)

        total = rr[k, me].astype(jnp.float32) + rr[k, line].astype(jnp.float32) + partial_hidden(me, k)
        packed = (total * gelu_slope[k]).astype(jnp.bfloat16)
        picked = dot(place[...], packed, 0, 0).astype(jnp.bfloat16)
        inc[k] = picked.reshape(dps, cap, width)
        here = ga_hbm.at[:, pl.ds(pl.multiple_of(d * hidden + k * width, 128), width)]
        for e in mates:
            remote(inc.at[k, e], here, ga_send, ga_recv, at(me, side, e)).start()
        pltpu.make_async_copy(inc.at[k, d], here, ga_recv).start()

    def weight_half(k, s):
        return dot(acts[k].reshape(line * rows, width), gz[s].reshape(line * rows, cols), 0, 0)

    def send_half(k):
        gs[k] = weight_half(k, other).astype(jnp.bfloat16)
        remote(gs.at[k], gr.at[k], gr_send, gr_recv.at[k], partner).start()

    def finish_weight(k):
        own = weight_half(k, side)
        await_bytes(gr.at[k], gr_recv.at[k])
        total = own + gr[k].astype(jnp.float32)
        stp[d] += jnp.sum(total * res[k], axis=0, keepdims=True)
        sl[k] = total * sl[k]
        pltpu.make_async_copy(
            sl.at[k], gw_hbm.at[pl.ds(pl.multiple_of(k * width, 16), width), :], gw_sem
        ).start()

    def when_chunk(k, act):
        @pl.when((k >= 0) & (k < K))
        def _():
            act(k)

    def await_grads():
        for z in range(line):
            await_bytes(gz.at[:, z, pl.ds(0, dps - 1)], ogd_recv.at[z])

    depth = LAG * (line - 1)

    def turn(t, carry):
        when_chunk(t, pack)

        for h in range(1, line):
            when_chunk(t - LAG * h, lambda k, h=h: hop(k, h))

        @pl.when(t == BEHIND)
        def _():
            await_grads()

        when_chunk(t - BEHIND, lambda k: await_bytes(qw.at[other, k], qw_recv.at[k]))
        when_chunk(t - BEHIND - LAG * me, sum_right)
        when_chunk(t - BEHIND - LAG * (line - 1 - me), sum_left)

        @pl.when(t + AHEAD < K)
        def _():
            send_acts(t + AHEAD)

        @pl.when(t + 1 < K)
        def _():
            quantize(t + 1)

        when_chunk(t - BEHIND - depth, finish_hidden)
        when_chunk(t - depth, send_half)
        when_chunk(t - depth - LAG, finish_weight)

        @pl.when(t == K - 1 + depth + LAG)
        def _():
            for e in mates:
                remote(stp.at[d], stp.at[d], st_send, st_recv, at(me, side, e)).start()

        return carry

    lax.fori_loop(0, K + depth + max(LAG, BEHIND), turn, 0)

    await_bytes(stp.at[pl.ds(0, dps - 1)], st_recv)
    total = stp[0]
    for e in range(1, dps):
        total = total + stp[e]
    gstep_ref[...] = ((FF_W * top_level) ** (-0.5)) * total

    await_bytes(stp.at[pl.ds(0, dps - 1)], st_send)
    await_bytes(slot_all.at[pl.ds(0, dps - 1)], slot_send)
    await_bytes(gz.at[:, pl.ds(0, line - 1), 0], ogz_send)
    await_bytes(gz.at[:, :, pl.ds(0, dps - 1)], ogd_send)
    await_bytes(inc.at[:, pl.ds(0, dps - 1)], inc_send)
    await_bytes(qw.at[0], qw_send)
    await_bytes(gs, gr_send)
    await_bytes(rr.at[:, pl.ds(0, line - 1)], rs_send)

    @pl.when((me == 0) | (me == line - 1))
    def _():
        await_bytes(acts.at[:, 0], ag_send)

    @pl.when((me > 0) & (me < line - 1))
    def _():
        await_bytes(rr, ag_send)

    await_bytes(inc.at[:, pl.ds(0, dps - 1)], ga_send)
    await_bytes(inc, ga_recv)
    await_bytes(sl, gw_sem)


def shards(patch_acts, patch_slot, out_grads, latent_weight, step_size):
    dps = lax.axis_size("dp")
    line = lax.axis_size("fsdp") // 2
    cap, features = patch_acts.shape
    hidden = features // dps
    own_rows, all_columns = out_grads.shape
    rows = own_rows * dps
    cols = latent_weight.shape[1]
    K = min(CHUNKS, hidden // 128)
    width = hidden // K
    grads = out_grads.reshape(own_rows, line, 2, cols).transpose(1, 2, 0, 3)
    bf16, f32 = jnp.bfloat16, jnp.float32
    vmem = pl.BlockSpec(memory_space=pltpu.VMEM)
    hbm = pl.BlockSpec(memory_space=pl.ANY)
    dma = pltpu.SemaphoreType.DMA
    return pl.pallas_call(
        functools.partial(kernel, line, dps),
        out_shape=(
            jax.ShapeDtypeStruct((cap, features), bf16),
            jax.ShapeDtypeStruct((hidden, cols), f32),
            jax.ShapeDtypeStruct((1, cols), f32),
        ),
        in_specs=[hbm, vmem, vmem, vmem, vmem],
        out_specs=(hbm, hbm, vmem),
        scratch_shapes=[
            pltpu.VMEM((K, dps, cap, width), bf16),
            pltpu.VMEM((dps, 1, cap), jnp.int32),
            pltpu.VMEM((rows, dps * cap), bf16),
            pltpu.VMEM((K, line, rows, width), bf16),
            pltpu.VMEM((K, rows, width), f32),
            pltpu.VMEM((2, line, dps, own_rows, cols), bf16),
            pltpu.VMEM((2, K, width, cols), bf16),
            pltpu.VMEM((K, line + 1, rows, width), bf16),
            pltpu.VMEM((K, width, cols), f32),
            pltpu.VMEM((K, width, cols), f32),
            pltpu.VMEM((K, width, cols), bf16),
            pltpu.VMEM((K, width, cols), bf16),
            pltpu.VMEM((rows, width), f32),
            pltpu.VMEM((dps, 1, cols), f32),
            dma, dma, dma((line,)), dma, dma((line,)), dma, dma((K,)), dma,
            dma((K,)), dma, dma((K, line)), dma, dma((K, line + 1)), dma, dma((K,)), dma,
            dma, dma, dma, dma, dma,
        ],
        compiler_params=pltpu.CompilerParams(
            collective_id=0, has_side_effects=True, vmem_limit_bytes=60 * 1024 * 1024
        ),
        cost_estimate=pl.CostEstimate(
            flops=8 * line * rows * hidden * cols, bytes_accessed=4 * cap * features,
            transcendentals=0,
        ),
    )(patch_acts, patch_slot.reshape(1, cap), grads, latent_weight.reshape(K, width, cols), step_size)


def solution(mesh):
    return jax.shard_map(
        shards,
        mesh=mesh,
        in_specs=(
            P(("fsdp", "dp"), None),
            P(("fsdp", "dp")),
            P(("fsdp", "dp"), None),
            P("dp", "fsdp"),
            P(None, "fsdp"),
        ),
        out_specs=(P(("fsdp", "dp"), None), P("dp", "fsdp"), P(None, "fsdp")),
        check_vma=False,
    )
```

```python
import functools

import jax
import jax.numpy as jnp
from jax import lax
from jax.experimental import pallas as pl
from jax.experimental.pallas import tpu as pltpu
from jax.sharding import PartitionSpec as P

FF_W = 12288
CHUNKS = 12
LAG = 1
BEHIND = 2
AHEAD = 4
MESH = pl.DeviceIdType.MESH

top_level = 7.0
wobble = 0.9
two_pi = 6.283185307179586
pi = 3.141592653589793
inv_root_two = 0.7071067811865476
inv_root_tau = 0.3989422804014327


def gelu_pair(values):
    normal_cdf = 0.5 * (1.0 + lax.erf(values * inv_root_two))
    density = jnp.exp(-0.5 * values * values) * inv_root_tau
    return (values * normal_cdf, normal_cdf + values * density)


def sin_cos_turns(turns):
    angle = pi * (turns - jnp.floor(turns + 0.5))
    square = angle * angle
    s = -1.0 / 39916800.0
    for c in (1.0 / 362880.0, -1.0 / 5040.0, 1.0 / 120.0, -1.0 / 6.0, 1.0):
        s = s * square + c
    s = s * angle
    c = 1.0 / 479001600.0
    for k in (-1.0 / 3628800.0, 1.0 / 40320.0, -1.0 / 720.0, 1.0 / 24.0, -0.5, 1.0):
        c = c * square + k
    return 2.0 * s * c, 1.0 - 2.0 * s * s


def soft_quantize(weight, step, inv_step):
    ratio = weight * inv_step
    unit = jnp.tanh(ratio * (1.0 / top_level))
    clipped = top_level * unit
    sine, cosine = sin_cos_turns(clipped)
    quantized = clipped - (wobble / two_pi) * sine
    slope = (1.0 - wobble * cosine) * (1.0 - unit * unit)
    return (step * quantized, slope, quantized - ratio * slope)


def dot(left, right, left_dim, right_dim):
    return lax.dot_general(
        left, right, (((left_dim,), (right_dim,)), ((), ())), preferred_element_type=jnp.float32
    )


def kernel(
    line, dps, acts_hbm, slots_ref, og_ref, latent_ref, step_ref,
    ga_hbm, gw_hbm, gstep_ref,
    inc, slot_all, place, acts, gelu_slope, gz, qw, rr, sl, res, gs, gr, tmp, stp,
    slot_recv, slot_send, ogz_recv, ogz_send, ogd_recv, ogd_send, inc_recv, inc_send,
    qw_recv, qw_send, ag_recv, ag_send, rs_recv, rs_send, gr_recv, gr_send,
    ga_recv, ga_send, gw_sem, st_recv, st_send,
):
    K = inc.shape[0]
    cap, width = inc.shape[2], inc.shape[3]
    rows = acts.shape[2]
    own_rows, cols = og_ref.shape[2], og_ref.shape[3]
    hidden = K * width
    f = lax.axis_index("fsdp")
    d = lax.axis_index("dp")
    me = lax.div(f, 2)
    side = lax.rem(f, 2)
    other = 1 - side

    def at(z, s, e):
        return (z * 2 + s, e)

    partner = at(me, other, d)
    right = at(jnp.minimum(me + 1, line - 1), side, d)
    left = at(jnp.maximum(me - 1, 0), side, d)
    mates = [lax.rem(d + j, dps) for j in range(1, dps)]
    others = [lax.rem(me + j, line) for j in range(1, line)]

    def remote(src, dst, send, recv, device):
        return pltpu.make_async_remote_copy(
            src_ref=src, dst_ref=dst, send_sem=send, recv_sem=recv,
            device_id=device, device_id_type=MESH,
        )

    def await_bytes(ref, sem):
        pltpu.make_async_copy(ref, ref, sem).wait()

    barrier = pltpu.get_barrier_semaphore()
    for z in others:
        pl.semaphore_signal(barrier, inc=1, device_id=at(z, side, d), device_id_type=MESH)
    for e in mates:
        pl.semaphore_signal(barrier, inc=1, device_id=at(me, side, e), device_id_type=MESH)
    pl.semaphore_signal(barrier, inc=1, device_id=partner, device_id_type=MESH)
    pl.semaphore_wait(barrier, line + dps - 1)

    for z in others:
        remote(og_ref.at[z], gz.at[:, me, d], ogz_send, ogz_recv.at[me], at(z, side, d)).start()
    for e in mates:
        remote(slots_ref, slot_all.at[d], slot_send, slot_recv, at(me, side, e)).start()
    slot_all[d] = slots_ref[...]
    gz[:, me, d] = og_ref[me]

    def send_acts(k):
        for e in mates:
            src = acts_hbm.at[:, pl.ds(pl.multiple_of(e * hidden + k * width, 128), width)]
            remote(src, inc.at[k, d], inc_send, inc_recv.at[k], at(me, side, e)).start()
        src = acts_hbm.at[:, pl.ds(pl.multiple_of(d * hidden + k * width, 128), width)]
        pltpu.make_async_copy(src, inc.at[k, d], inc_recv.at[k]).start()

    def forward_grads(z):
        for e in mates:
            remote(gz.at[:, z, d], gz.at[:, z, d], ogd_send, ogd_recv.at[z], at(me, side, e)).start()

    step = step_ref[...].astype(jnp.float32)
    inv_step = 1.0 / step

    def quantize(k):
        block = 32

        def body(i, carry):
            part = pl.ds(pl.multiple_of(i * block, block), block)
            weight = latent_ref[k, part, :].astype(jnp.float32)
            q, slope, rest = soft_quantize(weight, step, inv_step)
            qw[side, k, part, :] = q.astype(jnp.bfloat16)
            sl[k, part, :] = slope
            res[k, part, :] = rest
            return carry

        lax.fori_loop(0, width // block, body, 0)
        remote(qw.at[side, k], qw.at[side, k], qw_send, qw_recv.at[k], partner).start()

    send_acts(0)
    forward_grads(me)
    stp[d] = jnp.zeros((1, cols), jnp.float32)
    quantize(0)
    await_bytes(slot_all.at[pl.ds(0, dps - 1)], slot_recv)
    for e in range(dps):
        place[:, e * cap:(e + 1) * cap] = (
            lax.broadcasted_iota(jnp.int32, (rows, cap), 0) == slot_all[e]
        ).astype(jnp.float32).astype(jnp.bfloat16)
    send_acts(1)
    for z in others:
        await_bytes(gz.at[:, z, d], ogz_recv.at[z])
        forward_grads(z)
    for k in range(2, min(AHEAD, K)):
        send_acts(k)

    def clear(k, slot):
        rr[k, slot] = jnp.zeros((rows, width), jnp.bfloat16)

    def grads_of(s, z):
        return gz[s, z].reshape(rows, cols)

    def partial_hidden(z, k):
        return dot(grads_of(0, z), qw[0, k], 1, 1) + dot(grads_of(1, z), qw[1, k], 1, 1)

    def pack(k):
        await_bytes(inc.at[k], inc_recv.at[k])
        tmp[...] = dot(place[...], inc[k].reshape(dps * cap, width), 1, 0)
        block = 32

        def body(i, carry):
            part = pl.ds(pl.multiple_of(i * block, block), block)
            act, slope = gelu_pair(tmp[part, :])
            acts[k, me, part, :] = act.astype(jnp.bfloat16)
            gelu_slope[k, part, :] = slope
            return carry

        lax.fori_loop(0, rows // block, body, 0)
        send_line(k, me, True, True)

    def send_line(k, z, to_right, to_left):
        block = acts.at[k, z]
        if to_right:
            @pl.when(me < line - 1)
            def _():
                remote(block, block, ag_send, ag_recv.at[k, z], right).start()
        if to_left:
            @pl.when(me > 0)
            def _():
                remote(block, block, ag_send, ag_recv.at[k, z], left).start()

    def hop(k, h):
        @pl.when(me - h >= 0)
        def _():
            z = me - h
            await_bytes(acts.at[k, z], ag_recv.at[k, z])
            send_line(k, z, True, False)

        @pl.when(me + h <= line - 1)
        def _():
            z = me + h
            await_bytes(acts.at[k, z], ag_recv.at[k, z])
            send_line(k, z, False, True)

    def sum_right(k):
        for j in range(line - 1, 0, -1):
            @pl.when(me + j <= line - 1)
            def _():
                z = me + j

                @pl.when(me > 0)
                def _():
                    await_bytes(rr.at[k, z], rs_recv.at[k, z])

                @pl.when(me == 0)
                def _():
                    clear(k, z)

                total = rr[k, z].astype(jnp.float32) + partial_hidden(z, k)
                rr[k, z] = total.astype(jnp.bfloat16)
                remote(rr.at[k, z], rr.at[k, z], rs_send, rs_recv.at[k, z], right).start()

    def sum_left(k):
        for j in range(line - 1, 0, -1):
            @pl.when(me - j >= 0)
            def _():
                z = me - j
                slot = line if j == 1 else z

                @pl.when(me < line - 1)
                def _():
                    await_bytes(rr.at[k, z], rs_recv.at[k, z])

                @pl.when(me == line - 1)
                def _():
                    clear(k, z)

                total = rr[k, z].astype(jnp.float32) + partial_hidden(z, k)
                rr[k, z] = total.astype(jnp.bfloat16)
                remote(rr.at[k, z], rr.at[k, slot], rs_send, rs_recv.at[k, slot], left).start()

    def finish_hidden(k):
        @pl.when(me > 0)
        def _():
            await_bytes(rr.at[k, me], rs_recv.at[k, me])

        @pl.when(me < line - 1)
        def _():
            await_bytes(rr.at[k, line], rs_recv.at[k, line])

        @pl.when(me == 0)
        def _():
            clear(k, me)

        @pl.when(me == line - 1)
        def _():
            clear(k, line)

        total = rr[k, me].astype(jnp.float32) + rr[k, line].astype(jnp.float32) + partial_hidden(me, k)
        packed = (total * gelu_slope[k]).astype(jnp.bfloat16)
        picked = dot(place[...], packed, 0, 0).astype(jnp.bfloat16)
        inc[k] = picked.reshape(dps, cap, width)
        here = ga_hbm.at[:, pl.ds(pl.multiple_of(d * hidden + k * width, 128), width)]
        for e in mates:
            remote(inc.at[k, e], here, ga_send, ga_recv, at(me, side, e)).start()
        pltpu.make_async_copy(inc.at[k, d], here, ga_recv).start()

    def weight_half(k, s):
        return dot(acts[k].reshape(line * rows, width), gz[s].reshape(line * rows, cols), 0, 0)

    def send_half(k):
        gs[k] = weight_half(k, other).astype(jnp.bfloat16)
        remote(gs.at[k], gr.at[k], gr_send, gr_recv.at[k], partner).start()

    def finish_weight(k):
        own = weight_half(k, side)
        await_bytes(gr.at[k], gr_recv.at[k])
        total = own + gr[k].astype(jnp.float32)
        stp[d] += jnp.sum(total * res[k], axis=0, keepdims=True)
        sl[k] = total * sl[k]
        pltpu.make_async_copy(
            sl.at[k], gw_hbm.at[pl.ds(pl.multiple_of(k * width, 16), width), :], gw_sem
        ).start()

    def when_chunk(k, act):
        @pl.when((k >= 0) & (k < K))
        def _():
            act(k)

    def await_grads():
        for z in range(line):
            await_bytes(gz.at[:, z, pl.ds(0, dps - 1)], ogd_recv.at[z])

    depth = LAG * (line - 1)

    def turn(t, carry):
        when_chunk(t, pack)

        for h in range(1, line):
            when_chunk(t - LAG * h, lambda k, h=h: hop(k, h))

        @pl.when(t == BEHIND)
        def _():
            await_grads()

        when_chunk(t - BEHIND, lambda k: await_bytes(qw.at[other, k], qw_recv.at[k]))
        when_chunk(t - BEHIND - LAG * me, sum_right)
        when_chunk(t - BEHIND - LAG * (line - 1 - me), sum_left)

        @pl.when(t + AHEAD < K)
        def _():
            send_acts(t + AHEAD)

        @pl.when(t + 1 < K)
        def _():
            quantize(t + 1)

        when_chunk(t - BEHIND - depth, finish_hidden)
        when_chunk(t - depth, send_half)
        when_chunk(t - depth - LAG, finish_weight)

        @pl.when(t == K - 1 + depth + LAG)
        def _():
            for e in mates:
                remote(stp.at[d], stp.at[d], st_send, st_recv, at(me, side, e)).start()

        return carry

    lax.fori_loop(0, K + depth + max(LAG, BEHIND), turn, 0)

    await_bytes(stp.at[pl.ds(0, dps - 1)], st_recv)
    total = stp[0]
    for e in range(1, dps):
        total = total + stp[e]
    gstep_ref[...] = ((FF_W * top_level) ** (-0.5)) * total

    await_bytes(stp.at[pl.ds(0, dps - 1)], st_send)
    await_bytes(slot_all.at[pl.ds(0, dps - 1)], slot_send)
    await_bytes(gz.at[:, pl.ds(0, line - 1), 0], ogz_send)
    await_bytes(gz.at[:, :, pl.ds(0, dps - 1)], ogd_send)
    await_bytes(inc.at[:, pl.ds(0, dps - 1)], inc_send)
    await_bytes(qw.at[0], qw_send)
    await_bytes(gs, gr_send)
    await_bytes(rr.at[:, pl.ds(0, line - 1)], rs_send)

    @pl.when((me == 0) | (me == line - 1))
    def _():
        await_bytes(acts.at[:, 0], ag_send)

    @pl.when((me > 0) & (me < line - 1))
    def _():
        await_bytes(rr, ag_send)

    await_bytes(inc.at[:, pl.ds(0, dps - 1)], ga_send)
    await_bytes(inc, ga_recv)
    await_bytes(sl, gw_sem)


def shards(patch_acts, patch_slot, out_grads, latent_weight, step_size):
    dps = lax.axis_size("dp")
    line = lax.axis_size("fsdp") // 2
    cap, features = patch_acts.shape
    hidden = features // dps
    own_rows, all_columns = out_grads.shape
    rows = own_rows * dps
    cols = latent_weight.shape[1]
    K = min(CHUNKS, hidden // 128)
    width = hidden // K
    grads = out_grads.reshape(own_rows, line, 2, cols).transpose(1, 2, 0, 3)
    bf16, f32 = jnp.bfloat16, jnp.float32
    vmem = pl.BlockSpec(memory_space=pltpu.VMEM)
    hbm = pl.BlockSpec(memory_space=pl.ANY)
    dma = pltpu.SemaphoreType.DMA
    return pl.pallas_call(
        functools.partial(kernel, line, dps),
        out_shape=(
            jax.ShapeDtypeStruct((cap, features), bf16),
            jax.ShapeDtypeStruct((hidden, cols), f32),
            jax.ShapeDtypeStruct((1, cols), f32),
        ),
        in_specs=[hbm, vmem, vmem, vmem, vmem],
        out_specs=(hbm, hbm, vmem),
        scratch_shapes=[
            pltpu.VMEM((K, dps, cap, width), bf16),
            pltpu.VMEM((dps, 1, cap), jnp.int32),
            pltpu.VMEM((rows, dps * cap), bf16),
            pltpu.VMEM((K, line, rows, width), bf16),
            pltpu.VMEM((K, rows, width), f32),
            pltpu.VMEM((2, line, dps, own_rows, cols), bf16),
            pltpu.VMEM((2, K, width, cols), bf16),
            pltpu.VMEM((K, line + 1, rows, width), bf16),
            pltpu.VMEM((K, width, cols), f32),
            pltpu.VMEM((K, width, cols), f32),
            pltpu.VMEM((K, width, cols), bf16),
            pltpu.VMEM((K, width, cols), bf16),
            pltpu.VMEM((rows, width), f32),
            pltpu.VMEM((dps, 1, cols), f32),
            dma, dma, dma((line,)), dma, dma((line,)), dma, dma((K,)), dma,
            dma((K,)), dma, dma((K, line)), dma, dma((K, line + 1)), dma, dma((K,)), dma,
            dma, dma, dma, dma, dma,
        ],
        compiler_params=pltpu.CompilerParams(
            collective_id=0, has_side_effects=True, vmem_limit_bytes=60 * 1024 * 1024
        ),
        cost_estimate=pl.CostEstimate(
            flops=8 * line * rows * hidden * cols, bytes_accessed=4 * cap * features,
            transcendentals=0,
        ),
    )(patch_acts, patch_slot.reshape(1, cap), grads, latent_weight.reshape(K, width, cols), step_size)


def solution(mesh):
    return jax.shard_map(
        shards,
        mesh=mesh,
        in_specs=(
            P(("fsdp", "dp"), None),
            P(("fsdp", "dp")),
            P(("fsdp", "dp"), None),
            P("dp", "fsdp"),
            P(None, "fsdp"),
        ),
        out_specs=(P(("fsdp", "dp"), None), P("dp", "fsdp"), P(None, "fsdp")),
        check_vma=False,
    )
```

```python
import functools

import jax
import jax.numpy as jnp
from jax import lax
from jax.experimental import pallas as pl
from jax.experimental.pallas import tpu as pltpu
from jax.sharding import PartitionSpec as P

FF_W = 12288
CHUNKS = 12
LAG = 1
BEHIND = 2
AHEAD = 4
MESH = pl.DeviceIdType.MESH

top_level = 7.0
wobble = 0.9
two_pi = 6.283185307179586
pi = 3.141592653589793
inv_root_two = 0.7071067811865476
inv_root_tau = 0.3989422804014327


def gelu_pair(values):
    normal_cdf = 0.5 * (1.0 + lax.erf(values * inv_root_two))
    density = jnp.exp(-0.5 * values * values) * inv_root_tau
    return (values * normal_cdf, normal_cdf + values * density)


def sin_cos_turns(turns):
    angle = pi * (turns - jnp.floor(turns + 0.5))
    square = angle * angle
    s = -1.0 / 39916800.0
    for c in (1.0 / 362880.0, -1.0 / 5040.0, 1.0 / 120.0, -1.0 / 6.0, 1.0):
        s = s * square + c
    s = s * angle
    c = 1.0 / 479001600.0
    for k in (-1.0 / 3628800.0, 1.0 / 40320.0, -1.0 / 720.0, 1.0 / 24.0, -0.5, 1.0):
        c = c * square + k
    return 2.0 * s * c, 1.0 - 2.0 * s * s


def soft_quantize(weight, step, inv_step):
    ratio = weight * inv_step
    unit = jnp.tanh(ratio * (1.0 / top_level))
    clipped = top_level * unit
    sine, cosine = sin_cos_turns(clipped)
    quantized = clipped - (wobble / two_pi) * sine
    slope = (1.0 - wobble * cosine) * (1.0 - unit * unit)
    return (step * quantized, slope, quantized - ratio * slope)


def dot(left, right, left_dim, right_dim):
    return lax.dot_general(
        left, right, (((left_dim,), (right_dim,)), ((), ())), preferred_element_type=jnp.float32
    )


def kernel(
    line, dps, acts_hbm, slots_ref, og_ref, latent_ref, step_ref,
    ga_hbm, gw_hbm, gstep_ref,
    inc, slot_all, place, picks, acts, gelu_slope, gz, qw, rr, sl, res, gs, gr, own, tmp, act, quant, stp,
    slot_recv, slot_send, ogz_recv, ogz_send, ogd_recv, ogd_send, inc_recv, inc_send,
    qw_recv, qw_send, ag_recv, ag_send, rs_recv, rs_send, gr_recv, gr_send,
    ga_recv, ga_send, gw_sem, st_recv, st_send,
):
    K = inc.shape[0]
    cap, width = inc.shape[2], inc.shape[3]
    rows = acts.shape[3]
    own_rows, cols = og_ref.shape[0], sl.shape[2]
    hidden = K * width
    f = lax.axis_index("fsdp")
    d = lax.axis_index("dp")
    me = lax.div(f, 2)
    side = lax.rem(f, 2)
    other = 1 - side

    def at(z, s, e):
        return (z * 2 + s, e)

    partner = at(me, other, d)
    right = at(jnp.minimum(me + 1, line - 1), side, d)
    left = at(jnp.maximum(me - 1, 0), side, d)
    mates = [lax.rem(d + j, dps) for j in range(1, dps)]
    others = [lax.rem(me + j, line) for j in range(1, line)]

    def remote(src, dst, send, recv, device):
        return pltpu.make_async_remote_copy(
            src_ref=src, dst_ref=dst, send_sem=send, recv_sem=recv,
            device_id=device, device_id_type=MESH,
        )

    def await_bytes(ref, sem):
        pltpu.make_async_copy(ref, ref, sem).wait()

    barrier = pltpu.get_barrier_semaphore()
    for z in others:
        pl.semaphore_signal(barrier, inc=1, device_id=at(z, side, d), device_id_type=MESH)
    for e in mates:
        pl.semaphore_signal(barrier, inc=1, device_id=at(me, side, e), device_id_type=MESH)
    pl.semaphore_signal(barrier, inc=1, device_id=partner, device_id_type=MESH)
    pl.semaphore_wait(barrier, line + dps - 1)

    def og_of(z):
        return og_ref.at[:, pl.ds(pl.multiple_of(z * 2 * cols, 128), 2 * cols)]

    for z in others:
        remote(og_of(z), gz.at[me, d], ogz_send, ogz_recv.at[me], at(z, side, d)).start()
    for e in mates:
        remote(slots_ref, slot_all.at[d], slot_send, slot_recv, at(me, side, e)).start()
    slot_all[d] = slots_ref[...]
    gz[me, d] = og_of(me)[...]

    def send_acts(k):
        for e in mates:
            src = acts_hbm.at[:, pl.ds(pl.multiple_of(e * hidden + k * width, 128), width)]
            remote(src, inc.at[k, d], inc_send, inc_recv.at[k], at(me, side, e)).start()
        src = acts_hbm.at[:, pl.ds(pl.multiple_of(d * hidden + k * width, 128), width)]
        pltpu.make_async_copy(src, inc.at[k, d], inc_recv.at[k]).start()

    def forward_grads(z):
        for e in mates:
            remote(gz.at[z, d], gz.at[z, d], ogd_send, ogd_recv.at[z], at(me, side, e)).start()

    step = step_ref[...].astype(jnp.float32)
    inv_step = 1.0 / step

    def qw_of(k, s):
        return qw.at[k, pl.ds(pl.multiple_of(s * cols, 128), cols)]

    def quantize(k):
        block = 32

        def body(i, carry):
            part = pl.ds(pl.multiple_of(i * block, block), block)
            weight = latent_ref[k, part, :].astype(jnp.float32)
            q, slope, rest = soft_quantize(weight, step, inv_step)
            quant[part, :] = q.astype(jnp.bfloat16)
            sl[k, part, :] = slope
            res[k, part, :] = rest
            return carry

        lax.fori_loop(0, width // block, body, 0)
        mine = qw_of(k, side)
        mine[...] = quant[...].T
        remote(mine, mine, qw_send, qw_recv.at[k], partner).start()

    send_acts(0)
    forward_grads(me)
    stp[d] = jnp.zeros((1, cols), jnp.float32)
    quantize(0)
    await_bytes(slot_all.at[pl.ds(0, dps - 1)], slot_recv)
    for e in range(dps):
        hit = (lax.broadcasted_iota(jnp.int32, (rows, cap), 0) == slot_all[e]).astype(jnp.float32)
        place[:, e * cap:(e + 1) * cap] = hit.astype(jnp.bfloat16)
        picks[e * cap:(e + 1) * cap, :] = hit.T.astype(jnp.bfloat16)
    send_acts(1)
    for z in others:
        await_bytes(gz.at[z, d], ogz_recv.at[z])
        forward_grads(z)
    for k in range(2, min(AHEAD, K)):
        send_acts(k)

    def clear(k, slot):
        rr[k, slot] = jnp.zeros((rows, width), jnp.bfloat16)

    def partial_hidden(z, k):
        return dot(gz[z].reshape(rows, 2 * cols), qw[k], 1, 0)

    def pack(k):
        await_bytes(inc.at[k], inc_recv.at[k])
        tmp[...] = dot(place[...], inc[k].reshape(dps * cap, width), 1, 0)
        block = 32

        def body(i, carry):
            part = pl.ds(pl.multiple_of(i * block, block), block)
            value, slope = gelu_pair(tmp[part, :])
            act[part, :] = value.astype(jnp.bfloat16)
            gelu_slope[k, part, :] = slope
            return carry

        lax.fori_loop(0, rows // block, body, 0)
        acts[k, me] = act[...].T
        send_line(k, me, True, True)

    def send_line(k, z, to_right, to_left):
        block = acts.at[k, z]
        if to_right:
            @pl.when(me < line - 1)
            def _():
                remote(block, block, ag_send, ag_recv.at[k, z], right).start()
        if to_left:
            @pl.when(me > 0)
            def _():
                remote(block, block, ag_send, ag_recv.at[k, z], left).start()

    def hop(k, h):
        @pl.when(me - h >= 0)
        def _():
            z = me - h
            await_bytes(acts.at[k, z], ag_recv.at[k, z])
            send_line(k, z, True, False)

        @pl.when(me + h <= line - 1)
        def _():
            z = me + h
            await_bytes(acts.at[k, z], ag_recv.at[k, z])
            send_line(k, z, False, True)

    def sum_right(k):
        for j in range(line - 1, 0, -1):
            @pl.when(me + j <= line - 1)
            def _():
                z = me + j

                @pl.when(me > 0)
                def _():
                    await_bytes(rr.at[k, z], rs_recv.at[k, z])

                @pl.when(me == 0)
                def _():
                    clear(k, z)

                total = rr[k, z].astype(jnp.float32) + partial_hidden(z, k)
                rr[k, z] = total.astype(jnp.bfloat16)
                remote(rr.at[k, z], rr.at[k, z], rs_send, rs_recv.at[k, z], right).start()

    def sum_left(k):
        for j in range(line - 1, 0, -1):
            @pl.when(me - j >= 0)
            def _():
                z = me - j
                slot = line if j == 1 else z

                @pl.when(me < line - 1)
                def _():
                    await_bytes(rr.at[k, z], rs_recv.at[k, z])

                @pl.when(me == line - 1)
                def _():
                    clear(k, z)

                total = rr[k, z].astype(jnp.float32) + partial_hidden(z, k)
                rr[k, z] = total.astype(jnp.bfloat16)
                remote(rr.at[k, z], rr.at[k, slot], rs_send, rs_recv.at[k, slot], left).start()

    def finish_hidden(k):
        @pl.when(me > 0)
        def _():
            await_bytes(rr.at[k, me], rs_recv.at[k, me])

        @pl.when(me < line - 1)
        def _():
            await_bytes(rr.at[k, line], rs_recv.at[k, line])

        @pl.when(me == 0)
        def _():
            clear(k, me)

        @pl.when(me == line - 1)
        def _():
            clear(k, line)

        total = rr[k, me].astype(jnp.float32) + rr[k, line].astype(jnp.float32) + partial_hidden(me, k)
        packed = (total * gelu_slope[k]).astype(jnp.bfloat16)
        picked = dot(picks[...], packed, 1, 0).astype(jnp.bfloat16)
        inc[k] = picked.reshape(dps, cap, width)
        here = ga_hbm.at[:, pl.ds(pl.multiple_of(d * hidden + k * width, 128), width)]
        for e in mates:
            remote(inc.at[k, e], here, ga_send, ga_recv, at(me, side, e)).start()
        pltpu.make_async_copy(inc.at[k, d], here, ga_recv).start()

    def send_half(k):
        gathered = jnp.concatenate([acts[k, z] for z in range(line)], axis=1)
        both = dot(gathered, gz[...].reshape(line * rows, 2 * cols), 1, 0)
        low, high = both[:, :cols], both[:, cols:]
        gs[k] = jnp.where(side == 0, high, low).astype(jnp.bfloat16)
        remote(gs.at[k], gr.at[k], gr_send, gr_recv.at[k], partner).start()
        own[lax.rem(k, LAG + 1)] = jnp.where(side == 0, low, high)

    def finish_weight(k):
        await_bytes(gr.at[k], gr_recv.at[k])
        total = own[lax.rem(k, LAG + 1)] + gr[k].astype(jnp.float32)
        stp[d] += jnp.sum(total * res[k], axis=0, keepdims=True)
        sl[k] = total * sl[k]
        pltpu.make_async_copy(
            sl.at[k], gw_hbm.at[pl.ds(pl.multiple_of(k * width, 16), width), :], gw_sem
        ).start()

    def when_chunk(k, act):
        @pl.when((k >= 0) & (k < K))
        def _():
            act(k)

    def await_grads():
        for z in range(line):
            await_bytes(gz.at[z, pl.ds(0, dps - 1)], ogd_recv.at[z])

    depth = LAG * (line - 1)

    def turn(t, carry):
        when_chunk(t, pack)

        for h in range(1, line):
            when_chunk(t - LAG * h, lambda k, h=h: hop(k, h))

        @pl.when(t == BEHIND)
        def _():
            await_grads()

        when_chunk(t - BEHIND, lambda k: await_bytes(qw_of(k, other), qw_recv.at[k]))
        when_chunk(t - BEHIND - LAG * me, sum_right)
        when_chunk(t - BEHIND - LAG * (line - 1 - me), sum_left)

        @pl.when(t + AHEAD < K)
        def _():
            send_acts(t + AHEAD)

        @pl.when(t + 1 < K)
        def _():
            quantize(t + 1)

        when_chunk(t - BEHIND - depth, finish_hidden)
        when_chunk(t - depth, send_half)
        when_chunk(t - depth - LAG, finish_weight)

        @pl.when(t == K - 1 + depth + LAG)
        def _():
            for e in mates:
                remote(stp.at[d], stp.at[d], st_send, st_recv, at(me, side, e)).start()

        return carry

    lax.fori_loop(0, K + depth + max(LAG, BEHIND), turn, 0)

    await_bytes(stp.at[pl.ds(0, dps - 1)], st_recv)
    total = stp[0]
    for e in range(1, dps):
        total = total + stp[e]
    gstep_ref[...] = ((FF_W * top_level) ** (-0.5)) * total

    await_bytes(stp.at[pl.ds(0, dps - 1)], st_send)
    await_bytes(slot_all.at[pl.ds(0, dps - 1)], slot_send)
    await_bytes(gz.at[pl.ds(0, line - 1), 0], ogz_send)
    await_bytes(gz.at[:, pl.ds(0, dps - 1)], ogd_send)
    await_bytes(inc.at[:, pl.ds(0, dps - 1)], inc_send)
    await_bytes(gs, qw_send)
    await_bytes(gs, gr_send)
    await_bytes(rr.at[:, pl.ds(0, line - 1)], rs_send)

    @pl.when((me == 0) | (me == line - 1))
    def _():
        await_bytes(rr.at[:, 0], ag_send)

    @pl.when((me > 0) & (me < line - 1))
    def _():
        await_bytes(rr, ag_send)

    await_bytes(inc.at[:, pl.ds(0, dps - 1)], ga_send)
    await_bytes(inc, ga_recv)
    await_bytes(sl, gw_sem)


def shards(patch_acts, patch_slot, out_grads, latent_weight, step_size):
    dps = lax.axis_size("dp")
    line = lax.axis_size("fsdp") // 2
    cap, features = patch_acts.shape
    hidden = features // dps
    own_rows, all_columns = out_grads.shape
    rows = own_rows * dps
    true_cols = latent_weight.shape[1]
    K = min(CHUNKS, hidden // 128)
    width = hidden // K
    spare = -true_cols % 128
    cols = true_cols + spare
    grads = out_grads
    if spare:
        grads = jnp.pad(
            out_grads.reshape(own_rows, 2 * line, true_cols), ((0, 0), (0, 0), (0, spare))
        ).reshape(own_rows, 2 * line * cols)
        latent_weight = jnp.pad(latent_weight, ((0, 0), (0, spare)))
        step_size = jnp.pad(step_size, ((0, 0), (0, spare)), constant_values=1)
    bf16, f32 = jnp.bfloat16, jnp.float32
    vmem = pl.BlockSpec(memory_space=pltpu.VMEM)
    hbm = pl.BlockSpec(memory_space=pl.ANY)
    dma = pltpu.SemaphoreType.DMA
    grad_acts, grad_weight, grad_step = pl.pallas_call(
        functools.partial(kernel, line, dps),
        out_shape=(
            jax.ShapeDtypeStruct((cap, features), bf16),
            jax.ShapeDtypeStruct((hidden, cols), f32),
            jax.ShapeDtypeStruct((1, cols), f32),
        ),
        in_specs=[hbm, vmem, vmem, vmem, vmem],
        out_specs=(hbm, hbm, vmem),
        scratch_shapes=[
            pltpu.VMEM((K, dps, cap, width), bf16),
            pltpu.VMEM((dps, 1, cap), jnp.int32),
            pltpu.VMEM((rows, dps * cap), bf16),
            pltpu.VMEM((dps * cap, rows), bf16),
            pltpu.VMEM((K, line, width, rows), bf16),
            pltpu.VMEM((K, rows, width), f32),
            pltpu.VMEM((line, dps, own_rows, 2 * cols), bf16),
            pltpu.VMEM((K, 2 * cols, width), bf16),
            pltpu.VMEM((K, line + 1, rows, width), bf16),
            pltpu.VMEM((K, width, cols), f32),
            pltpu.VMEM((K, width, cols), f32),
            pltpu.VMEM((K, width, cols), bf16),
            pltpu.VMEM((K, width, cols), bf16),
            pltpu.VMEM((LAG + 1, width, cols), f32),
            pltpu.VMEM((rows, width), f32),
            pltpu.VMEM((rows, width), bf16),
            pltpu.VMEM((width, cols), bf16),
            pltpu.VMEM((dps, 1, cols), f32),
            dma, dma, dma((line,)), dma, dma((line,)), dma, dma((K,)), dma,
            dma((K,)), dma, dma((K, line)), dma, dma((K, line + 1)), dma, dma((K,)), dma,
            dma, dma, dma, dma, dma,
        ],
        compiler_params=pltpu.CompilerParams(
            collective_id=0, has_side_effects=True, vmem_limit_bytes=60 * 1024 * 1024
        ),
        cost_estimate=pl.CostEstimate(
            flops=8 * line * rows * hidden * cols, bytes_accessed=4 * cap * features,
            transcendentals=0,
        ),
    )(patch_acts, patch_slot.reshape(1, cap), grads, latent_weight.reshape(K, width, cols), step_size)
    if spare:
        grad_weight, grad_step = grad_weight[:, :true_cols], grad_step[:, :true_cols]
    return grad_acts, grad_weight, grad_step


def solution(mesh):
    return jax.shard_map(
        shards,
        mesh=mesh,
        in_specs=(
            P(("fsdp", "dp"), None),
            P(("fsdp", "dp")),
            P(("fsdp", "dp"), None),
            P("dp", "fsdp"),
            P(None, "fsdp"),
        ),
        out_specs=(P(("fsdp", "dp"), None), P("dp", "fsdp"), P(None, "fsdp")),
        check_vma=False,
    )
```

```python
import functools

import jax
import jax.numpy as jnp
from jax import lax
from jax.experimental import pallas as pl
from jax.experimental.pallas import tpu as pltpu
from jax.sharding import PartitionSpec as P

FF_W = 12288
CHUNKS = 12
LAG = 1
BEHIND = 3
AHEAD = 4
MESH = pl.DeviceIdType.MESH

top_level = 7.0
wobble = 0.9
two_pi = 6.283185307179586
pi = 3.141592653589793
inv_root_two = 0.7071067811865476
inv_root_tau = 0.3989422804014327


def gelu_pair(values):
    normal_cdf = 0.5 * (1.0 + lax.erf(values * inv_root_two))
    density = jnp.exp(-0.5 * values * values) * inv_root_tau
    return (values * normal_cdf, normal_cdf + values * density)


def sin_cos_turns(turns):
    angle = pi * (turns - jnp.floor(turns + 0.5))
    square = angle * angle
    s = -1.0 / 39916800.0
    for c in (1.0 / 362880.0, -1.0 / 5040.0, 1.0 / 120.0, -1.0 / 6.0, 1.0):
        s = s * square + c
    s = s * angle
    c = 1.0 / 479001600.0
    for k in (-1.0 / 3628800.0, 1.0 / 40320.0, -1.0 / 720.0, 1.0 / 24.0, -0.5, 1.0):
        c = c * square + k
    return 2.0 * s * c, 1.0 - 2.0 * s * s


def soft_quantize(weight, step, inv_step):
    ratio = weight * inv_step
    unit = jnp.tanh(ratio * (1.0 / top_level))
    clipped = top_level * unit
    sine, cosine = sin_cos_turns(clipped)
    quantized = clipped - (wobble / two_pi) * sine
    slope = (1.0 - wobble * cosine) * (1.0 - unit * unit)
    return (step * quantized, slope, quantized - ratio * slope)


def dot(left, right, left_dim, right_dim):
    return lax.dot_general(
        left, right, (((left_dim,), (right_dim,)), ((), ())), preferred_element_type=jnp.float32
    )


def kernel(
    line, dps, acts_hbm, slots_ref, og_ref, latent_ref, step_ref,
    ga_hbm, gw_hbm, gstep_ref,
    inc, slot_all, place, picks, acts, gelu_slope, gz, qw, rr, sl, res, gs, gr, own, tmp, act, quant, stp,
    slot_recv, slot_send, ogz_recv, ogz_send, ogp_recv, ogd_recv, ogd_send, inc_recv, inc_send,
    qw_recv, qw_send, ag_recv, ag_send, rs_recv, rs_send, gr_recv, gr_send,
    ga_recv, ga_send, gw_sem, st_recv, st_send,
):
    K = inc.shape[0]
    cap, width = inc.shape[2], inc.shape[3]
    rows = acts.shape[3]
    own_rows, cols = og_ref.shape[0], sl.shape[2]
    hidden = K * width
    f = lax.axis_index("fsdp")
    d = lax.axis_index("dp")
    me = lax.div(f, 2)
    side = lax.rem(f, 2)
    other = 1 - side

    def at(z, s, e):
        return (z * 2 + s, e)

    partner = at(me, other, d)
    right = at(jnp.minimum(me + 1, line - 1), side, d)
    left = at(jnp.maximum(me - 1, 0), side, d)
    mates = [lax.rem(d + j, dps) for j in range(1, dps)]
    mate = d + 1 - 2 * lax.rem(d, 2)
    peers = [lax.rem(d + 2 * j, dps) for j in range(1, dps // 2)]
    others = [lax.rem(me + j, line) for j in range(1, line)]

    def remote(src, dst, send, recv, device):
        return pltpu.make_async_remote_copy(
            src_ref=src, dst_ref=dst, send_sem=send, recv_sem=recv,
            device_id=device, device_id_type=MESH,
        )

    def await_bytes(ref, sem):
        pltpu.make_async_copy(ref, ref, sem).wait()

    barrier = pltpu.get_barrier_semaphore()
    for z in others:
        pl.semaphore_signal(barrier, inc=1, device_id=at(z, side, d), device_id_type=MESH)
    for e in mates:
        pl.semaphore_signal(barrier, inc=1, device_id=at(me, side, e), device_id_type=MESH)
    pl.semaphore_signal(barrier, inc=1, device_id=partner, device_id_type=MESH)
    pl.semaphore_wait(barrier, line + dps - 1)

    def og_of(z):
        return og_ref.at[:, pl.ds(pl.multiple_of(z * 2 * cols, 128), 2 * cols)]

    for z in others:
        remote(og_of(z), gz.at[me, d], ogz_send, ogz_recv.at[me], at(z, side, d)).start()
    for e in mates:
        remote(slots_ref, slot_all.at[d], slot_send, slot_recv, at(me, side, e)).start()
    slot_all[d] = slots_ref[...]
    gz[me, d] = og_of(me)[...]

    def send_acts(k):
        for e in mates:
            src = acts_hbm.at[:, pl.ds(pl.multiple_of(e * hidden + k * width, 128), width)]
            remote(src, inc.at[k, d], inc_send, inc_recv.at[k], at(me, side, e)).start()
        src = acts_hbm.at[:, pl.ds(pl.multiple_of(d * hidden + k * width, 128), width)]
        pltpu.make_async_copy(src, inc.at[k, d], inc_recv.at[k]).start()

    def forward_grads(z):
        block = gz.at[z, d]
        for e in peers:
            remote(block, block, ogd_send, ogp_recv.at[z], at(me, side, e)).start()
        remote(block, block, ogd_send, ogd_recv.at[z], at(me, side, mate)).start()

    def relay_grads(z):
        await_bytes(gz.at[z, pl.ds(0, dps // 2 - 1)], ogp_recv.at[z])
        for e in peers:
            block = gz.at[z, e]
            remote(block, block, ogd_send, ogd_recv.at[z], at(me, side, mate)).start()

    step = step_ref[...].astype(jnp.float32)
    inv_step = 1.0 / step

    def qw_of(k, s):
        return qw.at[k, pl.ds(pl.multiple_of(s * cols, 128), cols)]

    def quantize(k):
        block = 32

        def body(i, carry):
            part = pl.ds(pl.multiple_of(i * block, block), block)
            weight = latent_ref[k, part, :].astype(jnp.float32)
            q, slope, rest = soft_quantize(weight, step, inv_step)
            quant[part, :] = q.astype(jnp.bfloat16)
            sl[k, part, :] = slope
            res[k, part, :] = rest
            return carry

        lax.fori_loop(0, width // block, body, 0)
        mine = qw_of(k, side)
        mine[...] = quant[...].T
        remote(mine, mine, qw_send, qw_recv.at[k], partner).start()

    send_acts(0)
    forward_grads(me)
    stp[d] = jnp.zeros((1, cols), jnp.float32)
    quantize(0)
    await_bytes(slot_all.at[pl.ds(0, dps - 1)], slot_recv)
    for e in range(dps):
        hit = (lax.broadcasted_iota(jnp.int32, (rows, cap), 0) == slot_all[e]).astype(jnp.float32)
        place[:, e * cap:(e + 1) * cap] = hit.astype(jnp.bfloat16)
        picks[e * cap:(e + 1) * cap, :] = hit.T.astype(jnp.bfloat16)
    send_acts(1)
    for z in others:
        await_bytes(gz.at[z, d], ogz_recv.at[z])
        forward_grads(z)
    for k in range(2, min(AHEAD, K)):
        send_acts(k)

    def clear(k, slot):
        rr[k, slot] = jnp.zeros((rows, width), jnp.bfloat16)

    def partial_hidden(z, k):
        return dot(gz[z].reshape(rows, 2 * cols), qw[k], 1, 0)

    def pack(k):
        await_bytes(inc.at[k], inc_recv.at[k])
        tmp[...] = dot(place[...], inc[k].reshape(dps * cap, width), 1, 0)
        block = 32

        def body(i, carry):
            part = pl.ds(pl.multiple_of(i * block, block), block)
            value, slope = gelu_pair(tmp[part, :])
            act[part, :] = value.astype(jnp.bfloat16)
            gelu_slope[k, part, :] = slope
            return carry

        lax.fori_loop(0, rows // block, body, 0)
        acts[k, me] = act[...].T
        send_line(k, me, True, True)

    def send_line(k, z, to_right, to_left):
        block = acts.at[k, z]
        if to_right:
            @pl.when(me < line - 1)
            def _():
                remote(block, block, ag_send, ag_recv.at[k, z], right).start()
        if to_left:
            @pl.when(me > 0)
            def _():
                remote(block, block, ag_send, ag_recv.at[k, z], left).start()

    def hop(k, h):
        @pl.when(me - h >= 0)
        def _():
            z = me - h
            await_bytes(acts.at[k, z], ag_recv.at[k, z])
            send_line(k, z, True, False)

        @pl.when(me + h <= line - 1)
        def _():
            z = me + h
            await_bytes(acts.at[k, z], ag_recv.at[k, z])
            send_line(k, z, False, True)

    def sum_right(k):
        for j in range(line - 1, 0, -1):
            @pl.when(me + j <= line - 1)
            def _():
                z = me + j

                @pl.when(me > 0)
                def _():
                    await_bytes(rr.at[k, z], rs_recv.at[k, z])

                @pl.when(me == 0)
                def _():
                    clear(k, z)

                total = rr[k, z].astype(jnp.float32) + partial_hidden(z, k)
                rr[k, z] = total.astype(jnp.bfloat16)
                remote(rr.at[k, z], rr.at[k, z], rs_send, rs_recv.at[k, z], right).start()

    def sum_left(k):
        for j in range(line - 1, 0, -1):
            @pl.when(me - j >= 0)
            def _():
                z = me - j
                slot = line if j == 1 else z

                @pl.when(me < line - 1)
                def _():
                    await_bytes(rr.at[k, z], rs_recv.at[k, z])

                @pl.when(me == line - 1)
                def _():
                    clear(k, z)

                total = rr[k, z].astype(jnp.float32) + partial_hidden(z, k)
                rr[k, z] = total.astype(jnp.bfloat16)
                remote(rr.at[k, z], rr.at[k, slot], rs_send, rs_recv.at[k, slot], left).start()

    def finish_hidden(k):
        @pl.when(me > 0)
        def _():
            await_bytes(rr.at[k, me], rs_recv.at[k, me])

        @pl.when(me < line - 1)
        def _():
            await_bytes(rr.at[k, line], rs_recv.at[k, line])

        @pl.when(me == 0)
        def _():
            clear(k, me)

        @pl.when(me == line - 1)
        def _():
            clear(k, line)

        total = rr[k, me].astype(jnp.float32) + rr[k, line].astype(jnp.float32) + partial_hidden(me, k)
        packed = (total * gelu_slope[k]).astype(jnp.bfloat16)
        picked = dot(picks[...], packed, 1, 0).astype(jnp.bfloat16)
        inc[k] = picked.reshape(dps, cap, width)
        here = ga_hbm.at[:, pl.ds(pl.multiple_of(d * hidden + k * width, 128), width)]
        for e in mates:
            remote(inc.at[k, e], here, ga_send, ga_recv, at(me, side, e)).start()
        pltpu.make_async_copy(inc.at[k, d], here, ga_recv).start()

    def send_half(k):
        gathered = jnp.concatenate([acts[k, z] for z in range(line)], axis=1)
        both = dot(gathered, gz[...].reshape(line * rows, 2 * cols), 1, 0)
        low, high = both[:, :cols], both[:, cols:]
        gs[k] = jnp.where(side == 0, high, low).astype(jnp.bfloat16)
        remote(gs.at[k], gr.at[k], gr_send, gr_recv.at[k], partner).start()
        own[lax.rem(k, LAG + 1)] = jnp.where(side == 0, low, high)

    def finish_weight(k):
        await_bytes(gr.at[k], gr_recv.at[k])
        total = own[lax.rem(k, LAG + 1)] + gr[k].astype(jnp.float32)
        stp[d] += jnp.sum(total * res[k], axis=0, keepdims=True)
        sl[k] = total * sl[k]
        pltpu.make_async_copy(
            sl.at[k], gw_hbm.at[pl.ds(pl.multiple_of(k * width, 16), width), :], gw_sem
        ).start()

    def when_chunk(k, act):
        @pl.when((k >= 0) & (k < K))
        def _():
            act(k)

    def await_grads():
        for z in range(line):
            await_bytes(gz.at[z, pl.ds(0, dps // 2)], ogd_recv.at[z])

    depth = LAG * (line - 1)

    def turn(t, carry):
        when_chunk(t, pack)

        @pl.when(t == 1)
        def _():
            for z in range(line):
                relay_grads(z)

        for h in range(1, line):
            when_chunk(t - LAG * h, lambda k, h=h: hop(k, h))

        @pl.when(t == BEHIND)
        def _():
            await_grads()

        when_chunk(t - BEHIND, lambda k: await_bytes(qw_of(k, other), qw_recv.at[k]))
        when_chunk(t - BEHIND - LAG * me, sum_right)
        when_chunk(t - BEHIND - LAG * (line - 1 - me), sum_left)

        @pl.when(t + AHEAD < K)
        def _():
            send_acts(t + AHEAD)

        @pl.when(t + 1 < K)
        def _():
            quantize(t + 1)

        when_chunk(t - BEHIND - depth, finish_hidden)
        when_chunk(t - depth, send_half)
        when_chunk(t - depth - LAG, finish_weight)

        @pl.when(t == K - 1 + depth + LAG)
        def _():
            for e in mates:
                remote(stp.at[d], stp.at[d], st_send, st_recv, at(me, side, e)).start()

        return carry

    lax.fori_loop(0, K + depth + max(LAG, BEHIND), turn, 0)

    await_bytes(stp.at[pl.ds(0, dps - 1)], st_recv)
    total = stp[0]
    for e in range(1, dps):
        total = total + stp[e]
    gstep_ref[...] = ((FF_W * top_level) ** (-0.5)) * total

    await_bytes(stp.at[pl.ds(0, dps - 1)], st_send)
    await_bytes(slot_all.at[pl.ds(0, dps - 1)], slot_send)
    await_bytes(gz.at[pl.ds(0, line - 1), 0], ogz_send)
    await_bytes(gz.at[:, pl.ds(0, dps - 1)], ogd_send)
    await_bytes(inc.at[:, pl.ds(0, dps - 1)], inc_send)
    await_bytes(gs, qw_send)
    await_bytes(gs, gr_send)
    await_bytes(rr.at[:, pl.ds(0, line - 1)], rs_send)

    @pl.when((me == 0) | (me == line - 1))
    def _():
        await_bytes(rr.at[:, 0], ag_send)

    @pl.when((me > 0) & (me < line - 1))
    def _():
        await_bytes(rr, ag_send)

    await_bytes(inc.at[:, pl.ds(0, dps - 1)], ga_send)
    await_bytes(inc, ga_recv)
    await_bytes(sl, gw_sem)


def shards(patch_acts, patch_slot, out_grads, latent_weight, step_size):
    dps = lax.axis_size("dp")
    line = lax.axis_size("fsdp") // 2
    cap, features = patch_acts.shape
    hidden = features // dps
    own_rows, all_columns = out_grads.shape
    rows = own_rows * dps
    true_cols = latent_weight.shape[1]
    K = min(CHUNKS, hidden // 128)
    width = hidden // K
    spare = -true_cols % 128
    cols = true_cols + spare
    grads = out_grads
    if spare:
        grads = jnp.pad(
            out_grads.reshape(own_rows, 2 * line, true_cols), ((0, 0), (0, 0), (0, spare))
        ).reshape(own_rows, 2 * line * cols)
        latent_weight = jnp.pad(latent_weight, ((0, 0), (0, spare)))
        step_size = jnp.pad(step_size, ((0, 0), (0, spare)), constant_values=1)
    bf16, f32 = jnp.bfloat16, jnp.float32
    vmem = pl.BlockSpec(memory_space=pltpu.VMEM)
    hbm = pl.BlockSpec(memory_space=pl.ANY)
    dma = pltpu.SemaphoreType.DMA
    grad_acts, grad_weight, grad_step = pl.pallas_call(
        functools.partial(kernel, line, dps),
        out_shape=(
            jax.ShapeDtypeStruct((cap, features), bf16),
            jax.ShapeDtypeStruct((hidden, cols), f32),
            jax.ShapeDtypeStruct((1, cols), f32),
        ),
        in_specs=[hbm, vmem, vmem, vmem, vmem],
        out_specs=(hbm, hbm, vmem),
        scratch_shapes=[
            pltpu.VMEM((K, dps, cap, width), bf16),
            pltpu.VMEM((dps, 1, cap), jnp.int32),
            pltpu.VMEM((rows, dps * cap), bf16),
            pltpu.VMEM((dps * cap, rows), bf16),
            pltpu.VMEM((K, line, width, rows), bf16),
            pltpu.VMEM((K, rows, width), f32),
            pltpu.VMEM((line, dps, own_rows, 2 * cols), bf16),
            pltpu.VMEM((K, 2 * cols, width), bf16),
            pltpu.VMEM((K, line + 1, rows, width), bf16),
            pltpu.VMEM((K, width, cols), f32),
            pltpu.VMEM((K, width, cols), f32),
            pltpu.VMEM((K, width, cols), bf16),
            pltpu.VMEM((K, width, cols), bf16),
            pltpu.VMEM((LAG + 1, width, cols), f32),
            pltpu.VMEM((rows, width), f32),
            pltpu.VMEM((rows, width), bf16),
            pltpu.VMEM((width, cols), bf16),
            pltpu.VMEM((dps, 1, cols), f32),
            dma, dma, dma((line,)), dma, dma((line,)), dma((line,)), dma, dma((K,)), dma,
            dma((K,)), dma, dma((K, line)), dma, dma((K, line + 1)), dma, dma((K,)), dma,
            dma, dma, dma, dma, dma,
        ],
        compiler_params=pltpu.CompilerParams(
            collective_id=0, has_side_effects=True, vmem_limit_bytes=60 * 1024 * 1024
        ),
        cost_estimate=pl.CostEstimate(
            flops=8 * line * rows * hidden * cols, bytes_accessed=4 * cap * features,
            transcendentals=0,
        ),
    )(patch_acts, patch_slot.reshape(1, cap), grads, latent_weight.reshape(K, width, cols), step_size)
    if spare:
        grad_weight, grad_step = grad_weight[:, :true_cols], grad_step[:, :true_cols]
    return grad_acts, grad_weight, grad_step


def solution(mesh):
    return jax.shard_map(
        shards,
        mesh=mesh,
        in_specs=(
            P(("fsdp", "dp"), None),
            P(("fsdp", "dp")),
            P(("fsdp", "dp"), None),
            P("dp", "fsdp"),
            P(None, "fsdp"),
        ),
        out_specs=(P(("fsdp", "dp"), None), P("dp", "fsdp"), P(None, "fsdp")),
        check_vma=False,
    )
```

```python
import functools

import jax
import jax.numpy as jnp
from jax import lax
from jax.experimental import pallas as pl
from jax.experimental.pallas import tpu as pltpu
from jax.sharding import PartitionSpec as P

FF_W = 12288
CHUNKS = 12
LAG = 1
BEHIND = 3
AHEAD = 4
MESH = pl.DeviceIdType.MESH

top_level = 7.0
wobble = 0.9
two_pi = 6.283185307179586
pi = 3.141592653589793
inv_root_two = 0.7071067811865476
inv_root_tau = 0.3989422804014327


def gelu_pair(values):
    normal_cdf = 0.5 * (1.0 + lax.erf(values * inv_root_two))
    density = jnp.exp(-0.5 * values * values) * inv_root_tau
    return (values * normal_cdf, normal_cdf + values * density)


def sin_cos_turns(turns):
    angle = pi * (turns - jnp.floor(turns + 0.5))
    square = angle * angle
    s = -1.0 / 39916800.0
    for c in (1.0 / 362880.0, -1.0 / 5040.0, 1.0 / 120.0, -1.0 / 6.0, 1.0):
        s = s * square + c
    s = s * angle
    c = 1.0 / 479001600.0
    for k in (-1.0 / 3628800.0, 1.0 / 40320.0, -1.0 / 720.0, 1.0 / 24.0, -0.5, 1.0):
        c = c * square + k
    return 2.0 * s * c, 1.0 - 2.0 * s * s


def soft_quantize(weight, step, inv_step):
    ratio = weight * inv_step
    unit = jnp.tanh(ratio * (1.0 / top_level))
    clipped = top_level * unit
    sine, cosine = sin_cos_turns(clipped)
    quantized = clipped - (wobble / two_pi) * sine
    slope = (1.0 - wobble * cosine) * (1.0 - unit * unit)
    return (step * quantized, slope, quantized - ratio * slope)


def dot(left, right, left_dim, right_dim):
    return lax.dot_general(
        left, right, (((left_dim,), (right_dim,)), ((), ())), preferred_element_type=jnp.float32
    )


def kernel(
    line, dps, acts_hbm, slots_ref, og_ref, latent_ref, step_ref,
    ga_hbm, gw_hbm, gstep_ref,
    inc, slot_all, place, picks, acts, gelu_slope, gz, qw, rr, sl, res, gs, gr, own, tmp, act, quant, stp,
    slot_recv, slot_send, ogz_recv, ogz_send, ogp_recv, ogd_recv, ogd_send, inc_recv, inc_send,
    qw_recv, qw_send, ag_recv, ag_send, rs_recv, rs_send, gr_recv, gr_send,
    ga_recv, ga_send, gw_sem, st_recv, st_send,
):
    K = inc.shape[0]
    cap, width = inc.shape[2], inc.shape[3]
    rows = acts.shape[3]
    own_rows, cols = og_ref.shape[0], sl.shape[2]
    hidden = K * width
    f = lax.axis_index("fsdp")
    d = lax.axis_index("dp")
    me = lax.div(f, 2)
    side = lax.rem(f, 2)
    other = 1 - side

    def at(z, s, e):
        return (z * 2 + s, e)

    partner = at(me, other, d)
    right = at(jnp.minimum(me + 1, line - 1), side, d)
    left = at(jnp.maximum(me - 1, 0), side, d)
    mates = [lax.rem(d + j, dps) for j in range(1, dps)]
    mate = d + 1 - 2 * lax.rem(d, 2)
    peers = [lax.rem(d + 2 * j, dps) for j in range(1, dps // 2)]
    others = [lax.rem(me + j, line) for j in range(1, line)]

    def remote(src, dst, send, recv, device):
        return pltpu.make_async_remote_copy(
            src_ref=src, dst_ref=dst, send_sem=send, recv_sem=recv,
            device_id=device, device_id_type=MESH,
        )

    def await_bytes(ref, sem):
        pltpu.make_async_copy(ref, ref, sem).wait()

    barrier = pltpu.get_barrier_semaphore()
    for z in others:
        pl.semaphore_signal(barrier, inc=1, device_id=at(z, side, d), device_id_type=MESH)
    for e in mates:
        pl.semaphore_signal(barrier, inc=1, device_id=at(me, side, e), device_id_type=MESH)
    pl.semaphore_signal(barrier, inc=1, device_id=partner, device_id_type=MESH)
    pl.semaphore_wait(barrier, line + dps - 1)

    def og_of(z):
        return og_ref.at[:, pl.ds(pl.multiple_of(z * 2 * cols, 128), 2 * cols)]

    for z in others:
        remote(og_of(z), gz.at[me, d], ogz_send, ogz_recv.at[me], at(z, side, d)).start()
    for e in mates:
        remote(slots_ref, slot_all.at[d], slot_send, slot_recv, at(me, side, e)).start()
    slot_all[d] = slots_ref[...]
    gz[me, d] = og_of(me)[...]

    def send_acts(k):
        for e in mates:
            src = acts_hbm.at[:, pl.ds(pl.multiple_of(e * hidden + k * width, 128), width)]
            remote(src, inc.at[k, d], inc_send, inc_recv.at[k], at(me, side, e)).start()
        src = acts_hbm.at[:, pl.ds(pl.multiple_of(d * hidden + k * width, 128), width)]
        pltpu.make_async_copy(src, inc.at[k, d], inc_recv.at[k]).start()

    def forward_grads(z):
        block = gz.at[z, d]
        for e in peers:
            remote(block, block, ogd_send, ogp_recv.at[z], at(me, side, e)).start()
        remote(block, block, ogd_send, ogd_recv.at[z], at(me, side, mate)).start()

    def relay_grads(z):
        await_bytes(gz.at[z, pl.ds(0, dps // 2 - 1)], ogp_recv.at[z])
        for e in peers:
            block = gz.at[z, e]
            remote(block, block, ogd_send, ogd_recv.at[z], at(me, side, mate)).start()

    step = step_ref[...].astype(jnp.float32)
    inv_step = 1.0 / step

    def qw_of(k, s):
        return qw.at[k, pl.ds(pl.multiple_of(s * cols, 128), cols)]

    def quantize(k):
        block = 32

        def body(i, carry):
            part = pl.ds(pl.multiple_of(i * block, block), block)
            weight = latent_ref[k, part, :].astype(jnp.float32)
            q, slope, rest = soft_quantize(weight, step, inv_step)
            quant[part, :] = q.astype(jnp.bfloat16)
            sl[k, part, :] = slope
            res[k, part, :] = rest
            return carry

        lax.fori_loop(0, width // block, body, 0)
        mine = qw_of(k, side)
        mine[...] = quant[...].T
        remote(mine, mine, qw_send, qw_recv.at[k], partner).start()

    send_acts(0)
    forward_grads(me)
    stp[d] = jnp.zeros((1, cols), jnp.float32)
    quantize(0)
    await_bytes(slot_all.at[pl.ds(0, dps - 1)], slot_recv)
    for e in range(dps):
        hit = (lax.broadcasted_iota(jnp.int32, (rows, cap), 0) == slot_all[e]).astype(jnp.float32)
        place[:, e * cap:(e + 1) * cap] = hit.astype(jnp.bfloat16)
        picks[e * cap:(e + 1) * cap, :] = hit.T.astype(jnp.bfloat16)
    send_acts(1)
    for z in others:
        await_bytes(gz.at[z, d], ogz_recv.at[z])
        forward_grads(z)
    for k in range(2, min(AHEAD, K)):
        send_acts(k)

    def clear(k, slot):
        rr[k, slot] = jnp.zeros((rows, width), jnp.bfloat16)

    def partial_hidden(z, k):
        return dot(gz[z].reshape(rows, 2 * cols), qw[k], 1, 0)

    def pack(k):
        await_bytes(inc.at[k], inc_recv.at[k])
        tmp[...] = dot(place[...], inc[k].reshape(dps * cap, width), 1, 0)
        block = 32

        def body(i, carry):
            part = pl.ds(pl.multiple_of(i * block, block), block)
            value, slope = gelu_pair(tmp[part, :])
            act[part, :] = value.astype(jnp.bfloat16)
            gelu_slope[k, part, :] = slope
            return carry

        lax.fori_loop(0, rows // block, body, 0)
        acts[k, me] = act[...].T
        send_line(k, me, True, True)

    def send_line(k, z, to_right, to_left):
        block = acts.at[k, z]
        if to_right:
            @pl.when(me < line - 1)
            def _():
                remote(block, block, ag_send, ag_recv.at[k, z], right).start()
        if to_left:
            @pl.when(me > 0)
            def _():
                remote(block, block, ag_send, ag_recv.at[k, z], left).start()

    def hop(k, h):
        @pl.when(me - h >= 0)
        def _():
            z = me - h
            await_bytes(acts.at[k, z], ag_recv.at[k, z])
            send_line(k, z, True, False)

        @pl.when(me + h <= line - 1)
        def _():
            z = me + h
            await_bytes(acts.at[k, z], ag_recv.at[k, z])
            send_line(k, z, False, True)

    def sum_right(k):
        for j in range(line - 1, 0, -1):
            @pl.when(me + j <= line - 1)
            def _():
                z = me + j
                part = partial_hidden(z, k)

                @pl.when(me > 0)
                def _():
                    await_bytes(rr.at[k, z], rs_recv.at[k, z])

                @pl.when(me == 0)
                def _():
                    clear(k, z)

                total = rr[k, z].astype(jnp.float32) + part
                rr[k, z] = total.astype(jnp.bfloat16)
                remote(rr.at[k, z], rr.at[k, z], rs_send, rs_recv.at[k, z], right).start()

    def sum_left(k):
        for j in range(line - 1, 0, -1):
            @pl.when(me - j >= 0)
            def _():
                z = me - j
                slot = line if j == 1 else z
                part = partial_hidden(z, k)

                @pl.when(me < line - 1)
                def _():
                    await_bytes(rr.at[k, z], rs_recv.at[k, z])

                @pl.when(me == line - 1)
                def _():
                    clear(k, z)

                total = rr[k, z].astype(jnp.float32) + part
                rr[k, z] = total.astype(jnp.bfloat16)
                remote(rr.at[k, z], rr.at[k, slot], rs_send, rs_recv.at[k, slot], left).start()

    def finish_hidden(k):
        part = partial_hidden(me, k)

        @pl.when(me > 0)
        def _():
            await_bytes(rr.at[k, me], rs_recv.at[k, me])

        @pl.when(me < line - 1)
        def _():
            await_bytes(rr.at[k, line], rs_recv.at[k, line])

        @pl.when(me == 0)
        def _():
            clear(k, me)

        @pl.when(me == line - 1)
        def _():
            clear(k, line)

        total = rr[k, me].astype(jnp.float32) + rr[k, line].astype(jnp.float32) + part
        packed = (total * gelu_slope[k]).astype(jnp.bfloat16)
        picked = dot(picks[...], packed, 1, 0).astype(jnp.bfloat16)
        inc[k] = picked.reshape(dps, cap, width)
        here = ga_hbm.at[:, pl.ds(pl.multiple_of(d * hidden + k * width, 128), width)]
        for e in mates:
            remote(inc.at[k, e], here, ga_send, ga_recv, at(me, side, e)).start()
        pltpu.make_async_copy(inc.at[k, d], here, ga_recv).start()

    def send_half(k):
        gathered = jnp.concatenate([acts[k, z] for z in range(line)], axis=1)
        both = dot(gathered, gz[...].reshape(line * rows, 2 * cols), 1, 0)
        low, high = both[:, :cols], both[:, cols:]
        gs[k] = jnp.where(side == 0, high, low).astype(jnp.bfloat16)
        remote(gs.at[k], gr.at[k], gr_send, gr_recv.at[k], partner).start()
        own[lax.rem(k, LAG + 1)] = jnp.where(side == 0, low, high)

    def finish_weight(k):
        await_bytes(gr.at[k], gr_recv.at[k])
        total = own[lax.rem(k, LAG + 1)] + gr[k].astype(jnp.float32)
        stp[d] += jnp.sum(total * res[k], axis=0, keepdims=True)
        sl[k] = total * sl[k]
        pltpu.make_async_copy(
            sl.at[k], gw_hbm.at[pl.ds(pl.multiple_of(k * width, 16), width), :], gw_sem
        ).start()

    def when_chunk(k, act):
        @pl.when((k >= 0) & (k < K))
        def _():
            act(k)

    def await_grads():
        for z in range(line):
            await_bytes(gz.at[z, pl.ds(0, dps // 2)], ogd_recv.at[z])

    depth = LAG * (line - 1)

    def turn(t, carry):
        when_chunk(t, pack)

        @pl.when(t == 1)
        def _():
            for z in range(line):
                relay_grads(z)

        for h in range(1, line):
            when_chunk(t - LAG * h, lambda k, h=h: hop(k, h))

        @pl.when(t == BEHIND)
        def _():
            await_grads()

        when_chunk(t - BEHIND, lambda k: await_bytes(qw_of(k, other), qw_recv.at[k]))
        when_chunk(t - BEHIND - LAG * me, sum_right)
        when_chunk(t - BEHIND - LAG * (line - 1 - me), sum_left)

        @pl.when(t + AHEAD < K)
        def _():
            send_acts(t + AHEAD)

        @pl.when(t + 1 < K)
        def _():
            quantize(t + 1)

        when_chunk(t - BEHIND - depth, finish_hidden)
        when_chunk(t - depth, send_half)
        when_chunk(t - depth - LAG, finish_weight)

        @pl.when(t == K - 1 + depth + LAG)
        def _():
            for e in mates:
                remote(stp.at[d], stp.at[d], st_send, st_recv, at(me, side, e)).start()

        return carry

    lax.fori_loop(0, K + depth + max(LAG, BEHIND), turn, 0)

    await_bytes(stp.at[pl.ds(0, dps - 1)], st_recv)
    total = stp[0]
    for e in range(1, dps):
        total = total + stp[e]
    gstep_ref[...] = ((FF_W * top_level) ** (-0.5)) * total

    await_bytes(stp.at[pl.ds(0, dps - 1)], st_send)
    await_bytes(slot_all.at[pl.ds(0, dps - 1)], slot_send)
    await_bytes(gz.at[pl.ds(0, line - 1), 0], ogz_send)
    await_bytes(gz.at[:, pl.ds(0, dps - 1)], ogd_send)
    await_bytes(inc.at[:, pl.ds(0, dps - 1)], inc_send)
    await_bytes(gs, qw_send)
    await_bytes(gs, gr_send)
    await_bytes(rr.at[:, pl.ds(0, line - 1)], rs_send)

    @pl.when((me == 0) | (me == line - 1))
    def _():
        await_bytes(rr.at[:, 0], ag_send)

    @pl.when((me > 0) & (me < line - 1))
    def _():
        await_bytes(rr, ag_send)

    await_bytes(inc.at[:, pl.ds(0, dps - 1)], ga_send)
    await_bytes(inc, ga_recv)
    await_bytes(sl, gw_sem)


def shards(patch_acts, patch_slot, out_grads, latent_weight, step_size):
    dps = lax.axis_size("dp")
    line = lax.axis_size("fsdp") // 2
    cap, features = patch_acts.shape
    hidden = features // dps
    own_rows, all_columns = out_grads.shape
    rows = own_rows * dps
    true_cols = latent_weight.shape[1]
    K = min(CHUNKS, hidden // 128)
    width = hidden // K
    spare = -true_cols % 128
    cols = true_cols + spare
    grads = out_grads
    if spare:
        grads = jnp.pad(
            out_grads.reshape(own_rows, 2 * line, true_cols), ((0, 0), (0, 0), (0, spare))
        ).reshape(own_rows, 2 * line * cols)
        latent_weight = jnp.pad(latent_weight, ((0, 0), (0, spare)))
        step_size = jnp.pad(step_size, ((0, 0), (0, spare)), constant_values=1)
    bf16, f32 = jnp.bfloat16, jnp.float32
    vmem = pl.BlockSpec(memory_space=pltpu.VMEM)
    hbm = pl.BlockSpec(memory_space=pl.ANY)
    dma = pltpu.SemaphoreType.DMA
    grad_acts, grad_weight, grad_step = pl.pallas_call(
        functools.partial(kernel, line, dps),
        out_shape=(
            jax.ShapeDtypeStruct((cap, features), bf16),
            jax.ShapeDtypeStruct((hidden, cols), f32),
            jax.ShapeDtypeStruct((1, cols), f32),
        ),
        in_specs=[hbm, vmem, vmem, vmem, vmem],
        out_specs=(hbm, hbm, vmem),
        scratch_shapes=[
            pltpu.VMEM((K, dps, cap, width), bf16),
            pltpu.VMEM((dps, 1, cap), jnp.int32),
            pltpu.VMEM((rows, dps * cap), bf16),
            pltpu.VMEM((dps * cap, rows), bf16),
            pltpu.VMEM((K, line, width, rows), bf16),
            pltpu.VMEM((K, rows, width), f32),
            pltpu.VMEM((line, dps, own_rows, 2 * cols), bf16),
            pltpu.VMEM((K, 2 * cols, width), bf16),
            pltpu.VMEM((K, line + 1, rows, width), bf16),
            pltpu.VMEM((K, width, cols), f32),
            pltpu.VMEM((K, width, cols), f32),
            pltpu.VMEM((K, width, cols), bf16),
            pltpu.VMEM((K, width, cols), bf16),
            pltpu.VMEM((LAG + 1, width, cols), f32),
            pltpu.VMEM((rows, width), f32),
            pltpu.VMEM((rows, width), bf16),
            pltpu.VMEM((width, cols), bf16),
            pltpu.VMEM((dps, 1, cols), f32),
            dma, dma, dma((line,)), dma, dma((line,)), dma((line,)), dma, dma((K,)), dma,
            dma((K,)), dma, dma((K, line)), dma, dma((K, line + 1)), dma, dma((K,)), dma,
            dma, dma, dma, dma, dma,
        ],
        compiler_params=pltpu.CompilerParams(
            collective_id=0, has_side_effects=True, vmem_limit_bytes=60 * 1024 * 1024
        ),
        cost_estimate=pl.CostEstimate(
            flops=8 * line * rows * hidden * cols, bytes_accessed=4 * cap * features,
            transcendentals=0,
        ),
    )(patch_acts, patch_slot.reshape(1, cap), grads, latent_weight.reshape(K, width, cols), step_size)
    if spare:
        grad_weight, grad_step = grad_weight[:, :true_cols], grad_step[:, :true_cols]
    return grad_acts, grad_weight, grad_step


def solution(mesh):
    return jax.shard_map(
        shards,
        mesh=mesh,
        in_specs=(
            P(("fsdp", "dp"), None),
            P(("fsdp", "dp")),
            P(("fsdp", "dp"), None),
            P("dp", "fsdp"),
            P(None, "fsdp"),
        ),
        out_specs=(P(("fsdp", "dp"), None), P("dp", "fsdp"), P(None, "fsdp")),
        check_vma=False,
    )
```
